256 devices in a mesh: stream: 8 (over z_lo, x), span: 32 (over z_hi, y, core).
Axes of the slice: x: 4, y: 4, z: 8 (z_hi: 4, z_lo: 2; z = z_hi * 2 + z_lo), core: 2. Of those that a mesh axis runs over, the one named last changes fastest.
Arguments:
- fields: float32 [1, 96, 384, 1024], P(None, 'stream', 'span'), may hold values from -6 to 6
Outputs:
- coefficients: float32 [1, 96, 384, 1024], P(None, 'stream', 'span')
The draws below stay inside these ranges and needn't reach their ends.
All inputs are finite; a program needn't handle non-finite values.
Results may differ from the reference program's by a relative error of at most 0.00002.
Values sent between devices are 32-bit elements; how exact they have to be, the bound alone decides.
No kernel may reach another device: no remote copies, remote signals or barrier semaphores. Data moves between devices by JAX's collectives and lax.ppermute only.
A program may use at most 128 MiB of HBM per device.

```python
import jax
import jax.numpy as jnp
from jax import lax

FIELDS = 1
NZ = 1024
NX = 96
NY = 384


def steps_of(key, extent, pieces, low, top_value):
    gain, own = 1.0, jax.random.fold_in(key, 6)
    for position, blocks in pieces:
        steps = jnp.exp(jax.random.uniform(jax.random.fold_in(own, position), (blocks,), jnp.float32, low / len(pieces), top_value / len(pieces)))
        gain = gain * jnp.repeat(steps, extent[position] // blocks).reshape([-1 if axis == position else 1 for axis in range(len(extent))])
    return gain


def scatter_about(stream_key, dims, deviation, most, shards=(), held_as=jnp.bfloat16):
    entries = jax.random.normal(stream_key, dims, jnp.float32) * deviation
    if len(shards) > 0:
        entries = steps_of(stream_key, dims, shards, -0.22, 0.18) * entries
    return jnp.clip(entries, min=-most, max=most).astype(held_as)


def setup_inputs(seed: int = 0) -> dict:
    key_list = jax.random.split(jax.random.key(seed), 2)
    return {
        "fields": scatter_about(key_list[0], (FIELDS, NX, NY, NZ), 1.0, 6.0, ((1, 8), (2, 32)), jnp.float32),
    }


def take(array, axis, start, stop, step=1):
    return lax.slice_in_dim(array, start, stop, step, axis)


def lift_ext(ext, axis):
    pairs = (ext.shape[axis] - 12) // 2
    evens = take(ext, axis, 0, ext.shape[axis], 2)
    odds = take(ext, axis, 1, ext.shape[axis], 2)
    detail = take(odds, axis, 1, pairs + 4) - (0.5625 * (take(evens, axis, 1, pairs + 4) + take(evens, axis, 2, pairs + 5)) - 0.0625 * (take(evens, axis, 0, pairs + 3) + take(evens, axis, 3, pairs + 6)))
    smooth = take(evens, axis, 3, pairs + 3) + (0.28125 * (take(detail, axis, 1, pairs + 1) + take(detail, axis, 2, pairs + 2)) - 0.03125 * (take(detail, axis, 0, pairs) + take(detail, axis, 3, pairs + 3)))
    kept = take(detail, axis, 2, pairs + 2)
    joined = jnp.stack([smooth, kept], axis + 1)
    shape = list(smooth.shape)
    shape[axis] = 2 * pairs
    return joined.reshape(shape)


def wrap_local(array, axis):
    length = array.shape[axis]
    return jnp.concatenate([take(array, axis, length - 6, length), array, take(array, axis, 0, 6)], axis)


def level(array):
    for axis in (1, 2, 3):
        array = lift_ext(wrap_local(array, axis), axis)
    return array


def reference(fields):
    first = level(fields)
    coarse = level(first[:, ::2, ::2, ::2])
    return first.at[:, ::2, ::2, ::2].set(coarse)
```

```python
import functools

import jax
import jax.numpy as jnp
from jax import lax
from jax.experimental import pallas as pl
from jax.experimental.pallas import tpu as pltpu
from jax.sharding import PartitionSpec as P

NEAR_D, FAR_D = 0.5625, 0.0625
NEAR_S, FAR_S = 0.28125, 0.03125
PLANES, ROWS, CELLS, LANES = 12, 12, 1024, 128
TILES = CELLS // LANES
PAIRS = ROWS // 2


def total(a, b):
    return b if a is None else a if b is None else a + b


def scaled(factor, a):
    return None if a is None else factor * a


def near_far(near, far, a, b, c, d):
    return total(scaled(near, total(a, b)), scaled(far, total(c, d)))


def lift(left, cells, right):
    pairs = len(cells) // 2
    e = {i: cells[2 * i] for i in range(pairs)}
    o = {i: cells[2 * i + 1] for i in range(pairs)}
    if left is not None:
        o[-2], e[-1], o[-1] = left
    if right is not None:
        e[pairs], o[pairs], e[pairs + 1] = right
    d = {
        j: total(o.get(j), near_far(-NEAR_D, FAR_D, e.get(j), e.get(j + 1), e.get(j - 1), e.get(j + 2)))
        for j in range(-2, pairs + 1)
    }
    s = [
        total(e[i], near_far(NEAR_S, -FAR_S, d[i - 1], d[i], d[i - 2], d[i + 1]))
        for i in range(pairs)
    ]
    return s, [d[i] for i in range(pairs)]


def edge_right(c):
    return [
        total(c[-3], near_far(-NEAR_D, FAR_D, c[-4], None, c[-6], None)),
        c[-2],
        total(c[-1], scaled(FAR_D, c[-4])),
    ]


def edge_left(c):
    return [c[0], total(c[1], scaled(FAR_D, c[4])), c[2]]


def coarse_terms(c):
    zeros = [None] * len(c)
    to_right, _ = lift(edge_right(c), zeros, None)
    to_left, _ = lift(None, zeros, edge_left(c))
    return to_right, to_left


def plus(a, b):
    return [total(x, y) for x, y in zip(a, b)]


def interleaved(s, d):
    return [row for pair in zip(s, d) for row in pair]


def lane(shape):
    return lax.broadcasted_iota(jnp.int32, shape, len(shape) - 1)


def lift_lanes(v, step):
    n = v.shape[-1]
    at = lane(v.shape) & (2 * step - 1)
    roll = lambda x, k: pltpu.roll(x, (k * step) % n, axis=v.ndim - 1)
    d = v - (NEAR_D * (roll(v, 1) + roll(v, -1)) - FAR_D * (roll(v, 3) + roll(v, -3)))
    w = jnp.where(at == step, d, v)
    s = w + (NEAR_S * (roll(w, 1) + roll(w, -1)) - FAR_S * (roll(w, 3) + roll(w, -3)))
    return jnp.where(at == 0, s, w)


def packed(a, b):
    return jnp.where((lane(a.shape) & 1) == 0, a, pltpu.roll(b, 1, axis=b.ndim - 1))


def unpacked_odd(p):
    return pltpu.roll(p, p.shape[-1] - 1, axis=p.ndim - 1)


def cut(t):
    return pl.ds(t * LANES, LANES)


Y_ROWS, Y_FAR, X_ROWS, X_FAR = 56, 16, 56, 8


def span_edges(a_ref, b_ref, t):
    a = [a_ref[t, pl.ds(y, PLANES, stride=16), :] for y in range(ROWS)]
    b = [b_ref[t, pl.ds(y, PAIRS, stride=16), :] for y in range(ROWS)]
    return a, b


def put_rows(ref, start, rows, t):
    for row in rows:
        ref[pl.ds(start, row.shape[0]), cut(t)] = row
        start += row.shape[0]
    return start


def first_kernel(f_ref, a_ref, b_ref, near_ref, other_ref, far_ref):
    odd_core = lax.axis_index("span") % 2 == 1
    for k in range(PAIRS):
        lows = []
        for x in (2 * k, 2 * k + 1):
            a = lift_lanes(f_ref[x], 1)
            lows.append(lift_lanes(a, 2))
            for t in range(TILES):
                a_ref[t, pl.ds(x * 16, ROWS), :] = a[:, t * LANES:(t + 1) * LANES]
        b = packed(*lows)
        for t in range(TILES):
            b_ref[t, pl.ds(k * 16, ROWS), :] = b[:, t * LANES:(t + 1) * LANES]
    for t in range(TILES):
        a, b = span_edges(a_ref, b_ref, t)
        smooth, _ = lift(None, b, None)
        to_right, to_left = coarse_terms(b)
        far_right = edge_right(to_right)
        far_left = edge_left(to_left)
        sends_right = edge_right(a) + edge_right(smooth)
        sends_left = edge_left(a) + edge_left(smooth)
        near = [jnp.where(odd_core, l, r) for l, r in zip(sends_left, sends_right)]
        other = [jnp.where(odd_core, r, l) for l, r in zip(sends_left, sends_right)]
        far_right, far_left = [far_right[0], far_right[2]], [far_left[1], jnp.zeros_like(far_left[1])]
        end = put_rows(near_ref, 0, near, t)
        put_rows(near_ref, end, [jnp.where(odd_core, l, r) for l, r in zip(far_left, far_right)], t)
        put_rows(other_ref, 0, other, t)
        put_rows(far_ref, 0, [jnp.where(odd_core, r, l) for l, r in zip(far_left, far_right)], t)


def fold_kernel(other_ref, near_ref, out_ref):
    odd_core = lax.axis_index("span") % 2 == 1
    out_ref[...] = other_ref[...]
    for t in range(TILES):
        one = near_ref[pl.ds(54, PAIRS), cut(t)]
        two = near_ref[pl.ds(60, PAIRS), cut(t)]
        zero = jnp.zeros_like(one)
        for row, term in ((0, jnp.where(odd_core, one, zero)), (1, jnp.where(odd_core, zero, one)), (2, jnp.where(odd_core, two, zero))):
            at = pl.ds(36 + row * PAIRS, PAIRS)
            out_ref[at, cut(t)] = other_ref[at, cut(t)] + term


def middle_kernel(a_ref, b_ref, near_ref, other_ref, far_ref, ya_ref, yb_ref, right_ref, left_ref, right2_ref, left2_ref, halo_ref):
    odd_core = lax.axis_index("span") % 2 == 1
    for j in range(3):
        near = near_ref[pl.ds(12 * j, PLANES), :]
        other = other_ref[pl.ds(12 * j, PLANES), :]
        left = jnp.where(odd_core, near, other)
        right = jnp.where(odd_core, other, near)
        for side, h in ((0, left), (1, right)):
            low = lift_lanes(h, 2)
            for t in range(TILES):
                halo_ref[t, pl.ds((side * 3 + j) * 32, PLANES), :] = h[:, t * LANES:(t + 1) * LANES]
                halo_ref[t, pl.ds((side * 3 + j) * 32 + 16, PLANES), :] = low[:, t * LANES:(t + 1) * LANES]
    for t in range(TILES):
        a, b = span_edges(a_ref, b_ref, t)
        halo = [halo_ref[t, pl.ds(32 * j, PLANES), :] for j in range(6)]
        smooth, detail = lift(halo[:3], a, halo[3:])
        for c in range(PAIRS):
            ya_ref[t, pl.ds(c, PLANES, stride=16), :] = smooth[c]
            ya_ref[t, pl.ds(8 + c, PLANES, stride=16), :] = detail[c]
        low = [
            packed(halo_ref[t, pl.ds(32 * j + 16, PAIRS, stride=2), :], halo_ref[t, pl.ds(32 * j + 17, PAIRS, stride=2), :])
            for j in range(6)
        ]
        smooth, _ = lift(low[:3], b, low[3:])
        to_right, to_left = coarse_terms(b)
        near = [near_ref[pl.ds(36 + PAIRS * j, PAIRS), cut(t)] for j in range(3)]
        other = [other_ref[pl.ds(36 + PAIRS * j, PAIRS), cut(t)] for j in range(3)]
        far = [far_ref[pl.ds(PAIRS * j, PAIRS), cut(t)] for j in range(2)]
        left = [jnp.where(odd_core, n, o) for n, o in zip(near, other)]
        right = [jnp.where(odd_core, o, n) for n, o in zip(near, other)]
        zero = jnp.zeros_like(far[0])
        left = plus(plus(left, edge_right(to_left)), [jnp.where(odd_core, far[0], zero), None, jnp.where(odd_core, far[1], zero)])
        right = plus(plus(right, edge_left(to_right)), [None, jnp.where(odd_core, zero, far[0]), None])
        smooth, detail = lift(left, smooth, right)
        for c, row in enumerate(interleaved(smooth, detail)):
            yb_ref[t, pl.ds(c, PAIRS, stride=8), :] = row
    for t in range(TILES):
        a, b = stream_planes(ya_ref, yb_ref, t)
        smooth, _ = lift(None, b, None)
        to_right, to_left = coarse_terms(b)
        far_right, far_left = edge_right(to_right), edge_left(to_left)
        for ref, edge in ((right_ref, edge_right), (left_ref, edge_left)):
            end = 0
            for plane in edge(a):
                end = put_rows(ref, end, [plane[0:6], plane[8:14]], t)
            lows = edge(b) + edge(smooth)
            for j in range(3):
                end = put_rows(ref, end, [packed(lows[2 * j], lows[2 * j + 1])[0:6]], t)
        right2_ref[:, cut(t)] = packed(far_right[0], far_right[2])
        left2_ref[:, cut(t)] = far_left[1]


def stream_planes(ya_ref, yb_ref, t):
    a = [ya_ref[t, pl.ds(16 * x, 16), :] for x in range(PLANES)]
    b = []
    for k in range(PAIRS):
        pair = yb_ref[t, pl.ds(8 * k, 8), :]
        b += [pair, unpacked_odd(pair)]
    return a, b


def last_kernel(ya_ref, yb_ref, left_ref, right_ref, left2_ref, right2_ref, out_ref, la_ref, lb_ref, w_ref):
    even = (lane((8, LANES)) & 1) == 0
    for t in range(TILES):
        for side, ref in ((0, left_ref), (1, right_ref)):
            for j in range(3):
                la_ref[t, pl.ds((side * 3 + j) * 16, 6), :] = ref[pl.ds(12 * j, 6), cut(t)]
                la_ref[t, pl.ds((side * 3 + j) * 16 + 8, 6), :] = ref[pl.ds(12 * j + 6, 6), cut(t)]
                lb_ref[t, pl.ds((side * 3 + j) * 8, 6), :] = ref[pl.ds(36 + 6 * j, 6), cut(t)]
        a, b = stream_planes(ya_ref, yb_ref, t)
        halo = [la_ref[t, pl.ds(16 * j, 16), :] for j in range(6)]
        a_smooth, a_detail = lift(halo[:3], a, halo[3:])
        sides = []
        for side in (0, 1):
            pairs = [lb_ref[t, pl.ds((side * 3 + j) * 8, 8), :] for j in range(3)]
            sides.append([x for pair in pairs for x in (pair, unpacked_odd(pair))])
        smooth, _ = lift(sides[0][:3], b, sides[1][:3])
        to_right, to_left = coarse_terms(b)
        far_left = left2_ref[:, cut(t)]
        left = plus(plus(sides[0][3:], edge_right(to_left)), [far_left, None, unpacked_odd(far_left)])
        right = plus(plus(sides[1][3:], edge_left(to_right)), [None, right2_ref[:, cut(t)], None])
        coarse = interleaved(*lift(left, smooth, right))
        for k in range(PAIRS):
            for x, plane in ((2 * k, a_smooth[k]), (2 * k + 1, a_detail[k])):
                low, high = plane[0:8], plane[8:16]
                if x % 2 == 0:
                    low = jnp.where(even, coarse[k], low)
                w_ref[t, pl.ds(16 * x, 8, stride=2), :] = low
                w_ref[t, pl.ds(16 * x + 1, 8, stride=2), :] = high
        for x in range(PLANES):
            out_ref[x, :, t * LANES:(t + 1) * LANES] = w_ref[t, pl.ds(16 * x, ROWS), :]


VMEM = pl.BlockSpec(memory_space=pltpu.VMEM)


def call(kernel, shapes, args, scratch=()):
    return pl.pallas_call(
        kernel,
        out_shape=[jax.ShapeDtypeStruct(s, jnp.float32) for s in shapes],
        in_specs=[VMEM] * len(args),
        out_specs=[VMEM] * len(shapes),
        scratch_shapes=[pltpu.VMEM(s, jnp.float32) for s in scratch],
        compiler_params=pltpu.CompilerParams(vmem_limit_bytes=16 << 20),
    )(*args)


def local(streams, spans, fields):
    def send(message, target):
        pairs = [(s * spans + y, (lambda q: q[0] % streams * spans + q[1] % spans)(target(s, y))) for s in range(streams) for y in range(spans)]
        return lax.ppermute(message, ("stream", "span"), pairs)

    a, b, near, other, far = call(
        first_kernel,
        [(TILES, PLANES * 16, LANES), (TILES, PAIRS * 16, LANES), (72, CELLS), (Y_ROWS, CELLS), (Y_FAR, CELLS)],
        [fields.reshape(PLANES, ROWS, CELLS)],
    )
    near = send(near, lambda s, y: (s, y ^ 1))
    far = send(far, lambda s, y: (s, y + (2 if y % 2 else -2)))
    (other,) = call(fold_kernel, [(Y_ROWS, CELLS)], [other, near])
    other = send(other, lambda s, y: (s, y + (1 if y % 2 else -1)))
    ya, yb, right, left, right2, left2 = call(
        middle_kernel,
        [(TILES, PLANES * 16, LANES), (TILES, PAIRS * 8, LANES), (X_ROWS, CELLS), (X_ROWS, CELLS), (X_FAR, CELLS), (X_FAR, CELLS)],
        [a, b, near, other, far],
        [(TILES, 192, LANES)],
    )
    from_left = send(right, lambda s, y: (s + 1, y))
    from_right = send(left, lambda s, y: (s - 1, y))
    from_left2 = send(right2, lambda s, y: (s + 2, y))
    from_right2 = send(left2, lambda s, y: (s - 2, y))
    (out,) = call(
        last_kernel,
        [(PLANES, ROWS, CELLS)],
        [ya, yb, from_left, from_right, from_left2, from_right2],
        [(TILES, 96, LANES), (TILES, 48, LANES), (TILES, PLANES * 16, LANES)],
    )
    return out.reshape(fields.shape)


def solution(mesh):
    return jax.shard_map(
        functools.partial(local, mesh.shape["stream"], mesh.shape["span"]),
        mesh=mesh,
        in_specs=(P(None, "stream", "span", None),),
        out_specs=P(None, "stream", "span", None),
        check_vma=False,
    )
```

```python
import functools

import jax
import jax.numpy as jnp
import ml_dtypes
import numpy as np
from jax import lax
from jax.experimental import pallas as pl
from jax.experimental.pallas import tpu as pltpu
from jax.sharding import PartitionSpec as P

NEAR_D, FAR_D = 0.5625, 0.0625
NEAR_S, FAR_S = 0.28125, 0.03125
PLANES, ROWS, CELLS, LANES = 12, 12, 1024, 128
TILES = CELLS // LANES
PAIRS = ROWS // 2


def total(a, b):
    return b if a is None else a if b is None else a + b


def scaled(factor, a):
    return None if a is None else factor * a


def near_far(near, far, a, b, c, d):
    return total(scaled(near, total(a, b)), scaled(far, total(c, d)))


def lift(left, cells, right):
    pairs = len(cells) // 2
    e = {i: cells[2 * i] for i in range(pairs)}
    o = {i: cells[2 * i + 1] for i in range(pairs)}
    if left is not None:
        o[-2], e[-1], o[-1] = left
    if right is not None:
        e[pairs], o[pairs], e[pairs + 1] = right
    d = {
        j: total(o.get(j), near_far(-NEAR_D, FAR_D, e.get(j), e.get(j + 1), e.get(j - 1), e.get(j + 2)))
        for j in range(-2, pairs + 1)
    }
    s = [
        total(e[i], near_far(NEAR_S, -FAR_S, d[i - 1], d[i], d[i - 2], d[i + 1]))
        for i in range(pairs)
    ]
    return s, [d[i] for i in range(pairs)]


def edge_right(c):
    return [
        total(c[-3], near_far(-NEAR_D, FAR_D, c[-4], None, c[-6], None)),
        c[-2],
        total(c[-1], scaled(FAR_D, c[-4])),
    ]


def edge_left(c):
    return [c[0], total(c[1], scaled(FAR_D, c[4])), c[2]]


def coarse_terms(c):
    zeros = [None] * len(c)
    to_right, _ = lift(edge_right(c), zeros, None)
    to_left, _ = lift(None, zeros, edge_left(c))
    return to_right, to_left


def plus(a, b):
    return [total(x, y) for x, y in zip(a, b)]


def interleaved(s, d):
    return [row for pair in zip(s, d) for row in pair]


def lane(shape):
    return lax.broadcasted_iota(jnp.int32, shape, len(shape) - 1)


def band(size, step, first, count):
    v = np.eye(size)
    r = lambda k: np.roll(v, k * step, axis=1)
    at = np.arange(size) % (2 * step)
    d = v - (NEAR_D * (r(1) + r(-1)) - FAR_D * (r(3) + r(-3)))
    v = np.where(at == step, d, v)
    s = v + (NEAR_S * (r(1) + r(-1)) - FAR_S * (r(3) + r(-3)))
    v = np.where(at == 0, s, v)
    m = v[:, first:first + step * count:step]
    held = m.astype(ml_dtypes.bfloat16)
    assert (held.astype(np.float64) == m).all()
    return held


def parts(v):
    high = v.astype(jnp.bfloat16)
    rest = v - high.astype(jnp.float32)
    mid = rest.astype(jnp.bfloat16)
    return high, mid, (rest - mid.astype(jnp.float32)).astype(jnp.bfloat16)


def window(v, start, count):
    tiles = [(start + i) % TILES for i in range(count)]
    return jnp.concatenate([v[:, i * LANES:(i + 1) * LANES] for i in tiles], axis=1)


def banded(split, m, start, count):
    return sum(jnp.dot(window(p, start, count), m, preferred_element_type=jnp.float32) for p in split)


def cut(t):
    return pl.ds(t * LANES, LANES)


Y_ROWS, Y_FAR, X_ROWS, X_FAR = 56, 16, 56, 8


def span_edges(a_ref, b_ref, t):
    a = [a_ref[t, pl.ds(y, PLANES, stride=ROWS), :] for y in range(ROWS)]
    b = [b_ref[t, pl.ds(y, PAIRS, stride=ROWS), :] for y in range(ROWS)]
    return a, b


def put_rows(ref, start, rows, t):
    for row in rows:
        ref[pl.ds(start, row.shape[0]), cut(t)] = row
        start += row.shape[0]
    return start


def first_kernel(f_ref, fine_ref, low_ref, a_ref, b_ref, near_ref, other_ref, far_ref, v_ref):
    odd_core = lax.axis_index("span") % 2 == 1
    for x in range(PLANES):
        v_ref[pl.ds(x * ROWS, ROWS), :] = f_ref[x]
    split = parts(v_ref[...])
    for q in range(4):
        block = banded(split, fine_ref[...], 2 * q - 1, 4)
        v_ref[:, pl.ds(256 * q, 256)] = block
        for t in range(2):
            a_ref[2 * q + t] = block[:, t * LANES:(t + 1) * LANES]
    split = parts(v_ref[...])
    for q in range(2):
        v_ref[:, pl.ds(256 * q, 256)] = banded(split, low_ref[...], 4 * q - 1, 6)
    for t in range(TILES):
        for k in range(PAIRS):
            b_ref[t, pl.ds(k * ROWS, ROWS), :] = v_ref[pl.ds((2 * k + t // 4) * ROWS, ROWS), cut(t % 4)]
    for t in range(TILES):
        a, b = span_edges(a_ref, b_ref, t)
        smooth, _ = lift(None, b, None)
        to_right, to_left = coarse_terms(b)
        far_right = edge_right(to_right)
        far_left = edge_left(to_left)
        sends_right = edge_right(a) + edge_right(smooth)
        sends_left = edge_left(a) + edge_left(smooth)
        near = [jnp.where(odd_core, l, r) for l, r in zip(sends_left, sends_right)]
        other = [jnp.where(odd_core, r, l) for l, r in zip(sends_left, sends_right)]
        far_right, far_left = [far_right[0], far_right[2]], [far_left[1], jnp.zeros_like(far_left[1])]
        end = put_rows(near_ref, 0, near, t)
        put_rows(near_ref, end, [jnp.where(odd_core, l, r) for l, r in zip(far_left, far_right)], t)
        put_rows(other_ref, 0, other, t)
        put_rows(far_ref, 0, [jnp.where(odd_core, r, l) for l, r in zip(far_left, far_right)], t)


def fold_kernel(other_ref, near_ref, out_ref):
    odd_core = lax.axis_index("span") % 2 == 1
    out_ref[...] = other_ref[...]
    for t in range(TILES):
        one = near_ref[pl.ds(54, PAIRS), cut(t)]
        two = near_ref[pl.ds(60, PAIRS), cut(t)]
        zero = jnp.zeros_like(one)
        for row, term in ((0, jnp.where(odd_core, one, zero)), (1, jnp.where(odd_core, zero, one)), (2, jnp.where(odd_core, two, zero))):
            at = pl.ds(36 + row * PAIRS, PAIRS)
            out_ref[at, cut(t)] = other_ref[at, cut(t)] + term


def middle_kernel(a_ref, b_ref, near_ref, other_ref, far_ref, low_ref, ya_ref, yb_ref, right_ref, left_ref, right2_ref, left2_ref, halo_ref):
    odd_core = lax.axis_index("span") % 2 == 1
    for side, ref in ((0, near_ref), (1, other_ref)):
        split = parts(ref[pl.ds(0, 48), :])
        for q in range(2):
            low = banded(split, low_ref[...], 4 * q - 1, 6)
            for t in range(2):
                halo_ref[2 * q + t, pl.ds(side * 48, 48), :] = low[:, t * LANES:(t + 1) * LANES]
    for t in range(TILES):
        a, b = span_edges(a_ref, b_ref, t)
        near = [near_ref[pl.ds(PLANES * j, PLANES), cut(t)] for j in range(3)]
        other = [other_ref[pl.ds(PLANES * j, PLANES), cut(t)] for j in range(3)]
        left = [jnp.where(odd_core, n, o) for n, o in zip(near, other)]
        right = [jnp.where(odd_core, o, n) for n, o in zip(near, other)]
        smooth, detail = lift(left, a, right)
        for c in range(PAIRS):
            ya_ref[t, pl.ds(c, PLANES, stride=16), :] = smooth[c]
            ya_ref[t, pl.ds(8 + c, PLANES, stride=16), :] = detail[c]
        near, other = (
            [halo_ref[t % 4, pl.ds(48 * side + PLANES * j + t // 4, PAIRS, stride=2), :] for j in range(3)] for side in (0, 1)
        )
        left = [jnp.where(odd_core, n, o) for n, o in zip(near, other)]
        right = [jnp.where(odd_core, o, n) for n, o in zip(near, other)]
        smooth, _ = lift(left, b, right)
        to_right, to_left = coarse_terms(b)
        near = [near_ref[pl.ds(36 + PAIRS * j, PAIRS), cut(t)] for j in range(3)]
        other = [other_ref[pl.ds(36 + PAIRS * j, PAIRS), cut(t)] for j in range(3)]
        far = [far_ref[pl.ds(PAIRS * j, PAIRS), cut(t)] for j in range(2)]
        left = [jnp.where(odd_core, n, o) for n, o in zip(near, other)]
        right = [jnp.where(odd_core, o, n) for n, o in zip(near, other)]
        zero = jnp.zeros_like(far[0])
        left = plus(plus(left, edge_right(to_left)), [jnp.where(odd_core, far[0], zero), None, jnp.where(odd_core, far[1], zero)])
        right = plus(plus(right, edge_left(to_right)), [None, jnp.where(odd_core, zero, far[0]), None])
        smooth, detail = lift(left, smooth, right)
        for c, row in enumerate(interleaved(smooth, detail)):
            yb_ref[t, pl.ds(c, PAIRS, stride=8), :] = row
    for t in range(TILES):
        a = stream_planes(ya_ref, t)
        for ref, edge in ((right_ref, edge_right), (left_ref, edge_left)):
            end = 0
            for plane in edge(a):
                end = put_rows(ref, end, [plane[0:6], plane[8:14]], t)
    for t in range(4):
        b = low_planes(yb_ref, t)
        smooth, _ = lift(None, b, None)
        to_right, to_left = coarse_terms(b)
        far_right, far_left = edge_right(to_right), edge_left(to_left)
        for ref, edge in ((right_ref, edge_right), (left_ref, edge_left)):
            for half, planes in ((0, edge(b)), (4, edge(smooth))):
                put_rows(ref, 36, [plane[0:6] for plane in planes], t + half)
        right2_ref[:, cut(t)] = far_right[0]
        right2_ref[:, cut(t + 4)] = far_right[2]
        left2_ref[:, cut(t)] = far_left[1]


def stream_planes(ya_ref, t):
    return [ya_ref[t, pl.ds(16 * x, 16), :] for x in range(PLANES)]


def low_planes(yb_ref, t):
    return [yb_ref[t + 4 * odd, pl.ds(8 * k, 8), :] for k in range(PAIRS) for odd in (0, 1)]


def last_kernel(ya_ref, yb_ref, left_ref, right_ref, left2_ref, right2_ref, spread_ref, out_ref, la_ref, lb_ref, w_ref, c_ref):
    even = (lane((8, LANES)) & 1) == 0
    for t in range(4):
        b = low_planes(yb_ref, t)
        for side, ref in ((0, left_ref), (1, right_ref)):
            for j in range(3):
                for half in (0, 1):
                    lb_ref[t, pl.ds((side * 6 + half * 3 + j) * 8, 6), :] = ref[pl.ds(36 + 6 * j, 6), cut(t + 4 * half)]
        halo = [lb_ref[t, pl.ds(8 * j, 8), :] for j in range(12)]
        smooth, _ = lift(halo[0:3], b, halo[6:9])
        to_right, to_left = coarse_terms(b)
        left = plus(plus(halo[3:6], edge_right(to_left)), [left2_ref[:, cut(t)], None, left2_ref[:, cut(t + 4)]])
        right = plus(plus(halo[9:12], edge_left(to_right)), [None, right2_ref[:, cut(t)], None])
        for k, plane in enumerate(interleaved(*lift(left, smooth, right))):
            c_ref[pl.ds(8 * k, 8), cut(t)] = plane
    split = parts(c_ref[...])
    for t in range(TILES):
        for side, ref in ((0, left_ref), (1, right_ref)):
            for j in range(3):
                la_ref[t, pl.ds((side * 3 + j) * 16, 6), :] = ref[pl.ds(12 * j, 6), cut(t)]
                la_ref[t, pl.ds((side * 3 + j) * 16 + 8, 6), :] = ref[pl.ds(12 * j + 6, 6), cut(t)]
        if t % 2 == 0:
            spread = sum(
                jnp.dot(p[:, t * 64:t * 64 + LANES], spread_ref[...], preferred_element_type=jnp.float32) for p in split
            )
        coarse = spread[:, (t % 2) * LANES:(t % 2 + 1) * LANES]
        a = stream_planes(ya_ref, t)
        halo = [la_ref[t, pl.ds(16 * j, 16), :] for j in range(6)]
        a_smooth, a_detail = lift(halo[:3], a, halo[3:])
        for k in range(PAIRS):
            for x, plane in ((2 * k, a_smooth[k]), (2 * k + 1, a_detail[k])):
                low, high = plane[0:8], plane[8:16]
                if x % 2 == 0:
                    low = jnp.where(even, coarse[8 * k:8 * k + 8], low)
                w_ref[t, pl.ds(16 * x, 8, stride=2), :] = low
                w_ref[t, pl.ds(16 * x + 1, 8, stride=2), :] = high
        for x in range(PLANES):
            out_ref[x, :, t * LANES:(t + 1) * LANES] = w_ref[t, pl.ds(16 * x, ROWS), :]


VMEM = pl.BlockSpec(memory_space=pltpu.VMEM)


def call(kernel, shapes, args, scratch=()):
    return pl.pallas_call(
        kernel,
        out_shape=[jax.ShapeDtypeStruct(s, jnp.float32) for s in shapes],
        in_specs=[VMEM] * len(args),
        out_specs=[VMEM] * len(shapes),
        scratch_shapes=[pltpu.VMEM(s, jnp.float32) for s in scratch],
        compiler_params=pltpu.CompilerParams(vmem_limit_bytes=16 << 20),
    )(*args)


def local(streams, spans, fields):
    def send(message, target):
        pairs = [(s * spans + y, (lambda q: q[0] % streams * spans + q[1] % spans)(target(s, y))) for s in range(streams) for y in range(spans)]
        return lax.ppermute(message, ("stream", "span"), pairs)

    fine, low = jnp.asarray(band(512, 1, 128, 256)), jnp.asarray(band(768, 2, 128, 256))
    spread = jnp.asarray(np.repeat(np.eye(LANES), 2, axis=1) * (np.arange(2 * LANES) % 2 == 0), jnp.bfloat16)
    a, b, near, other, far = call(
        first_kernel,
        [(TILES, PLANES * ROWS, LANES), (TILES, PAIRS * ROWS, LANES), (72, CELLS), (Y_ROWS, CELLS), (Y_FAR, CELLS)],
        [fields.reshape(PLANES, ROWS, CELLS), fine, low],
        [(PLANES * ROWS, CELLS)],
    )
    near = send(near, lambda s, y: (s, y ^ 1))
    far = send(far, lambda s, y: (s, y + (2 if y % 2 else -2)))
    (other,) = call(fold_kernel, [(Y_ROWS, CELLS)], [other, near])
    other = send(other, lambda s, y: (s, y + (1 if y % 2 else -1)))
    ya, yb, right, left, right2, left2 = call(
        middle_kernel,
        [(TILES, PLANES * 16, LANES), (TILES, PAIRS * 8, LANES), (X_ROWS, CELLS), (X_ROWS, CELLS), (X_FAR, CELLS), (X_FAR, CELLS)],
        [a, b, near, other, far, low],
        [(4, 96, LANES)],
    )
    from_left = send(right, lambda s, y: (s + 1, y))
    from_right = send(left, lambda s, y: (s - 1, y))
    from_left2 = send(right2, lambda s, y: (s + 2, y))
    from_right2 = send(left2, lambda s, y: (s - 2, y))
    (out,) = call(
        last_kernel,
        [(PLANES, ROWS, CELLS)],
        [ya, yb, from_left, from_right, from_left2, from_right2, spread],
        [(TILES, 96, LANES), (4, 96, LANES), (TILES, PLANES * 16, LANES), (48, CELLS // 2)],
    )
    return out.reshape(fields.shape)


def solution(mesh):
    return jax.shard_map(
        functools.partial(local, mesh.shape["stream"], mesh.shape["span"]),
        mesh=mesh,
        in_specs=(P(None, "stream", "span", None),),
        out_specs=P(None, "stream", "span", None),
        check_vma=False,
    )
```

```python
import functools

import jax
import jax.numpy as jnp
import ml_dtypes
import numpy as np
from jax import lax
from jax.experimental import pallas as pl
from jax.experimental.pallas import tpu as pltpu
from jax.sharding import PartitionSpec as P

NEAR_D, FAR_D = 0.5625, 0.0625
NEAR_S, FAR_S = 0.28125, 0.03125
PLANES, ROWS, CELLS, LANES = 12, 12, 1024, 128
TILES = CELLS // LANES
PAIRS = ROWS // 2


def total(a, b):
    return b if a is None else a if b is None else a + b


def scaled(factor, a):
    return None if a is None else factor * a


def near_far(near, far, a, b, c, d):
    return total(scaled(near, total(a, b)), scaled(far, total(c, d)))


def lift(left, cells, right):
    pairs = len(cells) // 2
    e = {i: cells[2 * i] for i in range(pairs)}
    o = {i: cells[2 * i + 1] for i in range(pairs)}
    if left is not None:
        o[-2], e[-1], o[-1] = left
    if right is not None:
        e[pairs], o[pairs], e[pairs + 1] = right
    d = {
        j: total(o.get(j), near_far(-NEAR_D, FAR_D, e.get(j), e.get(j + 1), e.get(j - 1), e.get(j + 2)))
        for j in range(-2, pairs + 1)
    }
    s = [
        total(e[i], near_far(NEAR_S, -FAR_S, d[i - 1], d[i], d[i - 2], d[i + 1]))
        for i in range(pairs)
    ]
    return s, [d[i] for i in range(pairs)]


def edge_right(c):
    return [
        total(c[-3], near_far(-NEAR_D, FAR_D, c[-4], None, c[-6], None)),
        c[-2],
        total(c[-1], scaled(FAR_D, c[-4])),
    ]


def edge_left(c):
    return [c[0], total(c[1], scaled(FAR_D, c[4])), c[2]]


def coarse_terms(c):
    zeros = [None] * len(c)
    to_right, _ = lift(edge_right(c), zeros, None)
    to_left, _ = lift(None, zeros, edge_left(c))
    return to_right, to_left


def plus(a, b):
    return [total(x, y) for x, y in zip(a, b)]


def interleaved(s, d):
    return [row for pair in zip(s, d) for row in pair]


def lane(shape):
    return lax.broadcasted_iota(jnp.int32, shape, len(shape) - 1)


def band(size, step, first, count):
    v = np.eye(size)
    r = lambda k: np.roll(v, k * step, axis=1)
    at = np.arange(size) % (2 * step)
    d = v - (NEAR_D * (r(1) + r(-1)) - FAR_D * (r(3) + r(-3)))
    v = np.where(at == step, d, v)
    s = v + (NEAR_S * (r(1) + r(-1)) - FAR_S * (r(3) + r(-3)))
    v = np.where(at == 0, s, v)
    m = v[:, first:first + step * count:step]
    held = m.astype(ml_dtypes.bfloat16)
    assert (held.astype(np.float64) == m).all()
    return held


def parts(v):
    high = v.astype(jnp.bfloat16)
    rest = v - high.astype(jnp.float32)
    mid = rest.astype(jnp.bfloat16)
    return high, mid, (rest - mid.astype(jnp.float32)).astype(jnp.bfloat16)


def banded(tiles, m, start, count):
    chosen = [tiles[(start + i) % TILES] for i in range(count)]
    return sum(
        jnp.dot(jnp.concatenate(p, axis=1), m, preferred_element_type=jnp.float32) for p in zip(*chosen)
    )


def cut(t):
    return pl.ds(t * LANES, LANES)


NEAR, EDGE, Y_FAR, X_FAR = 66, 54, 12, 6


def at(count, t, start, size):
    return pl.ds(t * count + start, size)


def span_edges(a_ref, b_ref, t):
    a = [a_ref[t, pl.ds(y, PLANES, stride=ROWS), :] for y in range(ROWS)]
    b = [b_ref[t, pl.ds(y, PAIRS, stride=ROWS), :] for y in range(ROWS)]
    return a, b


def put_rows(ref, start, rows, t):
    count = ref.shape[0] // TILES
    for row in rows:
        ref[at(count, t, start, row.shape[0]), :] = row
        start += row.shape[0]
    return start


def get_rows(ref, start, size, number, t):
    count = ref.shape[0] // TILES
    return [ref[at(count, t, start + size * j, size), :] for j in range(number)]


def choose(odd, a, b):
    return [jnp.where(odd, x, y) for x, y in zip(a, b)]


def first_kernel(f_ref, fine_ref, low_ref, a_ref, b_ref, near_ref, other_ref, far_ref, in_ref, v_ref, sems):
    odd_core = lax.axis_index("span") % 2 == 1
    copies = []
    for g in range(4):
        rows = pl.ds(3 * g * ROWS * TILES, 3 * ROWS * TILES)
        copies.append(pltpu.make_async_copy(f_ref.at[rows], in_ref.at[rows], sems.at[g]))
        copies[-1].start()
    for copy in copies:
        copy.wait()
    tiles = [parts(in_ref[pl.ds(t, PLANES * ROWS, stride=TILES), :]) for t in range(TILES)]
    for q in range(4):
        block = banded(tiles, fine_ref[...], 2 * q - 1, 4)
        for t in range(2):
            a_ref[2 * q + t] = block[:, t * LANES:(t + 1) * LANES]
    tiles = [parts(a_ref[t]) for t in range(TILES)]
    for q in range(2):
        v_ref[:, pl.ds(256 * q, 256)] = banded(tiles, low_ref[...], 4 * q - 1, 6)
    for t in range(TILES):
        for k in range(PAIRS):
            b_ref[t, pl.ds(k * ROWS, ROWS), :] = v_ref[pl.ds((2 * k + t // 4) * ROWS, ROWS), cut(t % 4)]
    for t in range(TILES):
        a, b = span_edges(a_ref, b_ref, t)
        smooth, _ = lift(None, b, None)
        to_right, to_left = coarse_terms(b)
        far_right, far_left = edge_right(to_right), edge_left(to_left)
        far_right, far_left = [far_right[0], far_right[2]], [far_left[1], jnp.zeros_like(far_left[1])]
        right = edge_right(a) + edge_right(smooth)
        left = edge_left(a) + edge_left(smooth)
        put_rows(near_ref, 0, choose(odd_core, left + far_left, right + far_right), t)
        put_rows(other_ref, 0, choose(odd_core, right, left), t)
        put_rows(far_ref, 0, choose(odd_core, far_right, far_left), t)


def fold_kernel(other_ref, near_ref, out_ref):
    odd_core = lax.axis_index("span") % 2 == 1
    out_ref[...] = other_ref[...]
    for t in range(TILES):
        one, two = get_rows(near_ref, EDGE, PAIRS, 2, t)
        zero = jnp.zeros_like(one)
        terms = choose(odd_core, [one, zero, two], [zero, one, zero])
        put_rows(out_ref, 36, plus(get_rows(other_ref, 36, PAIRS, 3, t), terms), t)


def middle_kernel(a_ref, b_ref, near_ref, other_ref, far_ref, low_ref, ya_ref, yb_ref, xnear_ref, xother_ref, xfar_ref, xfar2_ref, halo_ref):
    odd_core = lax.axis_index("span") % 2 == 1
    odd_x = lax.axis_index("stream") % 2 == 1
    odd_pair = lax.axis_index("stream") // 2 % 2 == 1
    for side, ref in ((0, near_ref), (1, other_ref)):
        tiles = [parts(get_rows(ref, 0, 48, 1, t)[0]) for t in range(TILES)]
        for q in range(2):
            low = banded(tiles, low_ref[...], 4 * q - 1, 6)
            for t in range(2):
                halo_ref[2 * q + t, pl.ds(side * 48, 48), :] = low[:, t * LANES:(t + 1) * LANES]
    for t in range(TILES):
        a, b = span_edges(a_ref, b_ref, t)
        near, other = (get_rows(ref, 0, PLANES, 3, t) for ref in (near_ref, other_ref))
        smooth, detail = lift(choose(odd_core, near, other), a, choose(odd_core, other, near))
        for c in range(PAIRS):
            ya_ref[t, pl.ds(c, PLANES, stride=16), :] = smooth[c]
            ya_ref[t, pl.ds(8 + c, PLANES, stride=16), :] = detail[c]
        near, other = (
            [halo_ref[t % 4, pl.ds(48 * side + PLANES * j + t // 4, PAIRS, stride=2), :] for j in range(3)] for side in (0, 1)
        )
        smooth, _ = lift(choose(odd_core, near, other), b, choose(odd_core, other, near))
        to_right, to_left = coarse_terms(b)
        near, other = (get_rows(ref, 36, PAIRS, 3, t) for ref in (near_ref, other_ref))
        one, two = get_rows(far_ref, 0, PAIRS, 2, t)
        zero = jnp.zeros_like(one)
        left = plus(choose(odd_core, near, other), choose(odd_core, [one, zero, two], [zero, zero, zero]))
        right = plus(choose(odd_core, other, near), choose(odd_core, [zero, zero, zero], [zero, one, zero]))
        smooth, detail = lift(plus(left, edge_right(to_left)), smooth, plus(right, edge_left(to_right)))
        for c, row in enumerate(interleaved(smooth, detail)):
            yb_ref[t, pl.ds(c, PAIRS, stride=8), :] = row
    for t in range(TILES):
        a = stream_planes(ya_ref, t)
        right, left = edge_right(a), edge_left(a)
        for ref, planes in ((xnear_ref, choose(odd_x, left, right)), (xother_ref, choose(odd_x, right, left))):
            put_rows(ref, 0, [half for plane in planes for half in (plane[0:6], plane[8:14])], t)
    for t in range(4):
        b = low_planes(yb_ref, t)
        smooth, _ = lift(None, b, None)
        to_right, to_left = coarse_terms(b)
        for half, planes in ((0, b), (4, smooth)):
            right, left = edge_right(planes), edge_left(planes)
            put_rows(xnear_ref, 36, [plane[0:6] for plane in choose(odd_x, left, right)], t + half)
            put_rows(xother_ref, 36, [plane[0:6] for plane in choose(odd_x, right, left)], t + half)
        far_right, far_left = edge_right(to_right), edge_left(to_left)
        far_right, far_left = [far_right[0], far_right[2]], [far_left[1], jnp.zeros_like(far_left[1])]
        for half in (0, 1):
            put_rows(xfar_ref, 0, [choose(odd_pair, far_left, far_right)[half][0:6]], t + 4 * half)
            put_rows(xfar2_ref, 0, [choose(odd_pair, far_right, far_left)[half][0:6]], t + 4 * half)


def stream_planes(ya_ref, t):
    return [ya_ref[t, pl.ds(16 * x, 16), :] for x in range(PLANES)]


def low_planes(yb_ref, t):
    return [yb_ref[t + 4 * odd, pl.ds(8 * k, 8), :] for k in range(PAIRS) for odd in (0, 1)]


def last_kernel(ya_ref, yb_ref, xnear_ref, xother_ref, xfar_ref, xfar2_ref, spread_ref, out_ref, la_ref, lb_ref, c_ref, o_ref, sems):
    odd_x = lax.axis_index("stream") % 2 == 1
    odd_pair = lax.axis_index("stream") // 2 % 2 == 1
    even = (lane((8, LANES)) & 1) == 0
    for t in range(4):
        b = low_planes(yb_ref, t)
        near, other = (get_rows(ref, 36, 6, 3, t) + get_rows(ref, 36, 6, 3, t + 4) for ref in (xnear_ref, xother_ref))
        far, far2 = (get_rows(ref, 0, 6, 1, t) + get_rows(ref, 0, 6, 1, t + 4) for ref in (xfar_ref, xfar2_ref))
        rows = choose(odd_x, near, other) + choose(odd_x, other, near)
        rows += choose(odd_pair, far, far2) + choose(odd_pair, far2, far)[:1]
        for j, row in enumerate(rows):
            lb_ref[t, pl.ds(8 * j, 6), :] = row
        halo = [lb_ref[t, pl.ds(8 * j, 8), :] for j in range(15)]
        smooth, _ = lift(halo[0:3], b, halo[6:9])
        to_right, to_left = coarse_terms(b)
        left = plus(plus(halo[3:6], edge_right(to_left)), [halo[12], None, halo[13]])
        right = plus(plus(halo[9:12], edge_left(to_right)), [None, halo[14], None])
        for k, plane in enumerate(interleaved(*lift(left, smooth, right))):
            c_ref[pl.ds(8 * k, 8), cut(t)] = plane
    split = parts(c_ref[...])
    for t in range(TILES):
        near, other = (get_rows(ref, 0, 6, 6, t) for ref in (xnear_ref, xother_ref))
        for j, row in enumerate(choose(odd_x, near, other) + choose(odd_x, other, near)):
            la_ref[t, pl.ds(8 * j, 6), :] = row
        if t % 2 == 0:
            spread = sum(
                jnp.dot(p[:, t * 64:t * 64 + LANES], spread_ref[...], preferred_element_type=jnp.float32) for p in split
            )
        coarse = spread[:, (t % 2) * LANES:(t % 2 + 1) * LANES]
        a = stream_planes(ya_ref, t)
        halo = [la_ref[t, pl.ds(16 * j, 16), :] for j in range(6)]
        a_smooth, a_detail = lift(halo[:3], a, halo[3:])
        for k in range(PAIRS):
            for x, plane in ((2 * k, a_smooth[k]), (2 * k + 1, a_detail[k])):
                low, high = plane[0:8], plane[8:16]
                if x % 2 == 0:
                    low = jnp.where(even, coarse[8 * k:8 * k + 8], low)
                row = x * ROWS * TILES + t
                o_ref[pl.ds(row, PAIRS, stride=2 * TILES), :] = low[0:6]
                o_ref[pl.ds(row + TILES, PAIRS, stride=2 * TILES), :] = high[0:6]
    copies = []
    for g in range(4):
        rows = pl.ds(3 * g * ROWS * TILES, 3 * ROWS * TILES)
        copies.append(pltpu.make_async_copy(o_ref.at[rows], out_ref.at[rows], sems.at[g]))
        copies[-1].start()
    for copy in copies:
        copy.wait()


VMEM = pl.BlockSpec(memory_space=pltpu.VMEM)
HBM = pl.BlockSpec(memory_space=pltpu.HBM)


def call(kernel, shapes, args, scratch=(), sems=0, ins=VMEM, outs=VMEM):
    return pl.pallas_call(
        kernel,
        out_shape=[jax.ShapeDtypeStruct(s, jnp.float32) for s in shapes],
        in_specs=[ins] + [VMEM] * (len(args) - 1),
        out_specs=[outs] + [VMEM] * (len(shapes) - 1),
        scratch_shapes=[pltpu.VMEM(s, jnp.float32) for s in scratch] + [pltpu.SemaphoreType.DMA((sems,))] * (sems > 0),
        compiler_params=pltpu.CompilerParams(vmem_limit_bytes=16 << 20),
    )(*args)


def message(count):
    return (TILES * count, LANES)


def local(streams, spans, fields):
    def send(rows, target):
        pairs = [(s * spans + y, (lambda q: q[0] % streams * spans + q[1] % spans)(target(s, y))) for s in range(streams) for y in range(spans)]
        return lax.ppermute(rows, ("stream", "span"), pairs)

    fine, low = jnp.asarray(band(512, 1, 128, 256)), jnp.asarray(band(768, 2, 128, 256))
    spread = jnp.asarray(np.repeat(np.eye(LANES), 2, axis=1) * (np.arange(2 * LANES) % 2 == 0), jnp.bfloat16)
    block = (PLANES * ROWS * TILES, LANES)
    a, b, near, other, far = call(
        first_kernel,
        [(TILES, PLANES * ROWS, LANES), (TILES, PAIRS * ROWS, LANES), message(NEAR), message(EDGE), message(Y_FAR)],
        [fields.reshape(block), fine, low],
        [block, (PLANES * ROWS, CELLS)],
        sems=4,
        ins=HBM,
    )
    near = send(near, lambda s, y: (s, y ^ 1))
    far = send(far, lambda s, y: (s, y + (2 if y % 2 else -2)))
    (other,) = call(fold_kernel, [message(EDGE)], [other, near])
    other = send(other, lambda s, y: (s, y + (1 if y % 2 else -1)))
    ya, yb, xnear, xother, xfar, xfar2 = call(
        middle_kernel,
        [(TILES, PLANES * 16, LANES), (TILES, PAIRS * 8, LANES), message(EDGE), message(EDGE), message(X_FAR), message(X_FAR)],
        [a, b, near, other, far, low],
        [(4, 96, LANES)],
    )
    xnear = send(xnear, lambda s, y: (s ^ 1, y))
    xother = send(xother, lambda s, y: (s + (1 if s % 2 else -1), y))
    xfar = send(xfar, lambda s, y: (s + (-2 if s // 2 % 2 else 2), y))
    xfar2 = send(xfar2, lambda s, y: (s + (2 if s // 2 % 2 else -2), y))
    (out,) = call(
        last_kernel,
        [block],
        [ya, yb, xnear, xother, xfar, xfar2, spread],
        [(TILES, 96, LANES), (4, 120, LANES), (48, CELLS // 2), block],
        sems=4,
        outs=HBM,
    )
    return out.reshape(fields.shape)


def solution(mesh):
    return jax.shard_map(
        functools.partial(local, mesh.shape["stream"], mesh.shape["span"]),
        mesh=mesh,
        in_specs=(P(None, "stream", "span", None),),
        out_specs=P(None, "stream", "span", None),
        check_vma=False,
    )
```

```python
import functools

import jax
import jax.numpy as jnp
import ml_dtypes
import numpy as np
from jax import lax
from jax.experimental import pallas as pl
from jax.experimental.pallas import tpu as pltpu
from jax.sharding import PartitionSpec as P

NEAR_D, FAR_D = 0.5625, 0.0625
NEAR_S, FAR_S = 0.28125, 0.03125
PLANES, ROWS, CELLS, LANES = 12, 12, 1024, 128
TILES = CELLS // LANES
PAIRS = ROWS // 2


def total(a, b):
    return b if a is None else a if b is None else a + b


def scaled(factor, a):
    return None if a is None else factor * a


def near_far(near, far, a, b, c, d):
    return total(scaled(near, total(a, b)), scaled(far, total(c, d)))


def lift(left, cells, right):
    pairs = len(cells) // 2
    e = {i: cells[2 * i] for i in range(pairs)}
    o = {i: cells[2 * i + 1] for i in range(pairs)}
    if left is not None:
        o[-2], e[-1], o[-1] = left
    if right is not None:
        e[pairs], o[pairs], e[pairs + 1] = right
    d = {
        j: total(o.get(j), near_far(-NEAR_D, FAR_D, e.get(j), e.get(j + 1), e.get(j - 1), e.get(j + 2)))
        for j in range(-2, pairs + 1)
    }
    s = [
        total(e[i], near_far(NEAR_S, -FAR_S, d[i - 1], d[i], d[i - 2], d[i + 1]))
        for i in range(pairs)
    ]
    return s, [d[i] for i in range(pairs)]


def edge_right(c):
    return [
        total(c[-3], near_far(-NEAR_D, FAR_D, c[-4], None, c[-6], None)),
        c[-2],
        total(c[-1], scaled(FAR_D, c[-4])),
    ]


def edge_left(c):
    return [c[0], total(c[1], scaled(FAR_D, c[4])), c[2]]


def coarse_terms(c):
    zeros = [None] * len(c)
    to_right, _ = lift(edge_right(c), zeros, None)
    to_left, _ = lift(None, zeros, edge_left(c))
    return to_right, to_left


def plus(a, b):
    return [total(x, y) for x, y in zip(a, b)]


def interleaved(s, d):
    return [row for pair in zip(s, d) for row in pair]


def lane(shape):
    return lax.broadcasted_iota(jnp.int32, shape, len(shape) - 1)


def cut(t):
    return pl.ds(t * LANES, LANES)


def taps():
    v = np.eye(32)
    at = np.arange(32) % 2
    r = lambda k: np.roll(v, k, axis=1)
    v = np.where(at == 1, v - (NEAR_D * (r(1) + r(-1)) - FAR_D * (r(3) + r(-3))), v)
    v = np.where(at == 0, v + (NEAR_S * (r(1) + r(-1)) - FAR_S * (r(3) + r(-3))), v)
    assert (v == v.astype(ml_dtypes.bfloat16).astype(np.float64)).all()
    found = {k: (float(v[16 + k, 16]), float(v[17 + k, 17])) for k in range(-8, 9)}
    return {k: pair for k, pair in found.items() if any(pair)}


def table_kernel(fine_ref, low_ref):
    i, j = (lax.broadcasted_iota(jnp.int32, (LANES, LANES), axis) for axis in (0, 1))
    smooth = (j & 1) == 0
    value = {k: jnp.where(smooth, *pair) for k, pair in taps().items()}

    def block(step, tile):
        offset = i + tile * LANES - step * j
        out = jnp.zeros((LANES, LANES), jnp.float32)
        for k, v in value.items():
            out = jnp.where(offset == step * k, v, out)
        return out.astype(jnp.bfloat16)

    for ref, step in ((fine_ref, 1), (low_ref, 2)):
        ref[...] = jnp.zeros(ref.shape, jnp.bfloat16)
        for n in range(step + 2):
            one = block(step, n - 1)
            for column in (0, 1):
                ref[pl.ds((n + step * column) * LANES, LANES), cut(column)] = one


def parts(v):
    high = v.astype(jnp.bfloat16)
    rest = v - high.astype(jnp.float32)
    mid = rest.astype(jnp.bfloat16)
    return high, mid, (rest - mid.astype(jnp.float32)).astype(jnp.bfloat16)


def banded(tiles, m, start, count):
    chosen = [tiles[(start + i) % TILES] for i in range(count)]
    return sum(
        jnp.dot(jnp.concatenate(p, axis=1), m, preferred_element_type=jnp.float32) for p in zip(*chosen)
    )


NEAR, EDGE, Y_FAR, X_FAR = 66, 54, 12, 6


def at(count, t, start, size):
    return pl.ds(t * count + start, size)


def span_edges(a_ref, b_ref, t):
    a = [a_ref[t, pl.ds(y, PLANES, stride=ROWS), :] for y in range(ROWS)]
    b = [b_ref[t, pl.ds(y, PAIRS, stride=ROWS), :] for y in range(ROWS)]
    return a, b


def put_rows(ref, start, rows, t):
    count = ref.shape[0] // TILES
    for row in rows:
        ref[at(count, t, start, row.shape[0]), :] = row
        start += row.shape[0]
    return start


def get_rows(ref, start, size, number, t):
    count = ref.shape[0] // TILES
    return [ref[at(count, t, start + size * j, size), :] for j in range(number)]


def choose(odd, a, b):
    return [jnp.where(odd, x, y) for x, y in zip(a, b)]


def first_kernel(f_ref, fine_ref, low_ref, a_ref, b_ref, near_ref, other_ref, far_ref, v_ref):
    odd_core = lax.axis_index("span") % 2 == 1
    tiles = [parts(f_ref[pl.ds(t, PLANES * ROWS, stride=TILES), :]) for t in range(TILES)]
    for q in range(4):
        block = banded(tiles, fine_ref[...], 2 * q - 1, 4)
        for t in range(2):
            a_ref[2 * q + t] = block[:, t * LANES:(t + 1) * LANES]
    tiles = [parts(a_ref[t]) for t in range(TILES)]
    for q in range(2):
        v_ref[:, pl.ds(256 * q, 256)] = banded(tiles, low_ref[...], 4 * q - 1, 6)
    for t in range(TILES):
        for k in range(PAIRS):
            b_ref[t, pl.ds(k * ROWS, ROWS), :] = v_ref[pl.ds((2 * k + t // 4) * ROWS, ROWS), cut(t % 4)]
    for t in range(TILES):
        a, b = span_edges(a_ref, b_ref, t)
        smooth, _ = lift(None, b, None)
        to_right, to_left = coarse_terms(b)
        far_right, far_left = edge_right(to_right), edge_left(to_left)
        far_right, far_left = [far_right[0], far_right[2]], [far_left[1], jnp.zeros_like(far_left[1])]
        right = edge_right(a) + edge_right(smooth)
        left = edge_left(a) + edge_left(smooth)
        put_rows(near_ref, 0, choose(odd_core, left + far_left, right + far_right), t)
        put_rows(other_ref, 0, choose(odd_core, right, left), t)
        put_rows(far_ref, 0, choose(odd_core, far_right, far_left), t)


def fold_kernel(other_ref, near_ref, out_ref):
    odd_core = lax.axis_index("span") % 2 == 1
    out_ref[...] = other_ref[...]
    for t in range(TILES):
        one, two = get_rows(near_ref, EDGE, PAIRS, 2, t)
        zero = jnp.zeros_like(one)
        terms = choose(odd_core, [one, zero, two], [zero, one, zero])
        put_rows(out_ref, 36, plus(get_rows(other_ref, 36, PAIRS, 3, t), terms), t)


def middle_kernel(a_ref, b_ref, near_ref, other_ref, far_ref, low_ref, ya_ref, yb_ref, xnear_ref, xother_ref, xfar_ref, xfar2_ref, halo_ref):
    odd_core = lax.axis_index("span") % 2 == 1
    odd_x = lax.axis_index("stream") % 2 == 1
    odd_pair = lax.axis_index("stream") // 2 % 2 == 1
    for side, ref in ((0, near_ref), (1, other_ref)):
        tiles = [parts(get_rows(ref, 0, 48, 1, t)[0]) for t in range(TILES)]
        for q in range(2):
            low = banded(tiles, low_ref[...], 4 * q - 1, 6)
            for t in range(2):
                halo_ref[2 * q + t, pl.ds(side * 48, 48), :] = low[:, t * LANES:(t + 1) * LANES]
    for t in range(TILES):
        a, b = span_edges(a_ref, b_ref, t)
        near, other = (get_rows(ref, 0, PLANES, 3, t) for ref in (near_ref, other_ref))
        smooth, detail = lift(choose(odd_core, near, other), a, choose(odd_core, other, near))
        for c in range(PAIRS):
            ya_ref[t, pl.ds(c, PLANES, stride=16), :] = smooth[c]
            ya_ref[t, pl.ds(8 + c, PLANES, stride=16), :] = detail[c]
        near, other = (
            [halo_ref[t % 4, pl.ds(48 * side + PLANES * j + t // 4, PAIRS, stride=2), :] for j in range(3)] for side in (0, 1)
        )
        smooth, _ = lift(choose(odd_core, near, other), b, choose(odd_core, other, near))
        to_right, to_left = coarse_terms(b)
        near, other = (get_rows(ref, 36, PAIRS, 3, t) for ref in (near_ref, other_ref))
        one, two = get_rows(far_ref, 0, PAIRS, 2, t)
        zero = jnp.zeros_like(one)
        left = plus(choose(odd_core, near, other), choose(odd_core, [one, zero, two], [zero, zero, zero]))
        right = plus(choose(odd_core, other, near), choose(odd_core, [zero, zero, zero], [zero, one, zero]))
        smooth, detail = lift(plus(left, edge_right(to_left)), smooth, plus(right, edge_left(to_right)))
        for c, row in enumerate(interleaved(smooth, detail)):
            yb_ref[t, pl.ds(c, PAIRS, stride=8), :] = row
    for t in range(TILES):
        a = stream_planes(ya_ref, t)
        right, left = edge_right(a), edge_left(a)
        for ref, planes in ((xnear_ref, choose(odd_x, left, right)), (xother_ref, choose(odd_x, right, left))):
            put_rows(ref, 0, [half for plane in planes for half in (plane[0:6], plane[8:14])], t)
    for t in range(4):
        b = low_planes(yb_ref, t)
        smooth, _ = lift(None, b, None)
        to_right, to_left = coarse_terms(b)
        for half, planes in ((0, b), (4, smooth)):
            right, left = edge_right(planes), edge_left(planes)
            put_rows(xnear_ref, 36, [plane[0:6] for plane in choose(odd_x, left, right)], t + half)
            put_rows(xother_ref, 36, [plane[0:6] for plane in choose(odd_x, right, left)], t + half)
        far_right, far_left = edge_right(to_right), edge_left(to_left)
        far_right, far_left = [far_right[0], far_right[2]], [far_left[1], jnp.zeros_like(far_left[1])]
        for half in (0, 1):
            put_rows(xfar_ref, 0, [choose(odd_pair, far_left, far_right)[half][0:6]], t + 4 * half)
            put_rows(xfar2_ref, 0, [choose(odd_pair, far_right, far_left)[half][0:6]], t + 4 * half)


def stream_planes(ya_ref, t):
    return [ya_ref[t, pl.ds(16 * x, 16), :] for x in range(PLANES)]


def low_planes(yb_ref, t):
    return [yb_ref[t + 4 * odd, pl.ds(8 * k, 8), :] for k in range(PAIRS) for odd in (0, 1)]


def last_kernel(ya_ref, yb_ref, xnear_ref, xother_ref, xfar_ref, xfar2_ref, out_ref, la_ref, lb_ref, c_ref, o_ref, sems):
    odd_x = lax.axis_index("stream") % 2 == 1
    odd_pair = lax.axis_index("stream") // 2 % 2 == 1

    def rows_of(x, y, t):
        return pl.ds((x * ROWS + y) * TILES + t, PAIRS, stride=2 * TILES)

    def leave(x):
        rows = pl.ds(x * ROWS * TILES, ROWS * TILES)
        copy = pltpu.make_async_copy(o_ref.at[rows], out_ref.at[rows], sems.at[x])
        copy.start()
        return copy

    for t in range(TILES):
        near, other = (get_rows(ref, 0, 6, 6, t) for ref in (xnear_ref, xother_ref))
        for j, row in enumerate(choose(odd_x, near, other) + choose(odd_x, other, near)):
            la_ref[t, pl.ds(8 * j, 6), :] = row
        a = stream_planes(ya_ref, t)
        halo = [la_ref[t, pl.ds(16 * j, 16), :] for j in range(6)]
        for x, plane in enumerate(interleaved(*lift(halo[:3], a, halo[3:]))):
            o_ref[rows_of(x, 0, t), :] = plane[0:6]
            o_ref[rows_of(x, 1, t), :] = plane[8:14]
    copies = [leave(x) for x in range(1, PLANES, 2)]
    for t in range(4):
        b = low_planes(yb_ref, t)
        near, other = (get_rows(ref, 36, 6, 3, t) + get_rows(ref, 36, 6, 3, t + 4) for ref in (xnear_ref, xother_ref))
        far, far2 = (get_rows(ref, 0, 6, 1, t) + get_rows(ref, 0, 6, 1, t + 4) for ref in (xfar_ref, xfar2_ref))
        rows = choose(odd_x, near, other) + choose(odd_x, other, near)
        rows += choose(odd_pair, far, far2) + choose(odd_pair, far2, far)[:1]
        for j, row in enumerate(rows):
            lb_ref[t, pl.ds(8 * j, 6), :] = row
        halo = [lb_ref[t, pl.ds(8 * j, 8), :] for j in range(15)]
        smooth, _ = lift(halo[0:3], b, halo[6:9])
        to_right, to_left = coarse_terms(b)
        left = plus(plus(halo[3:6], edge_right(to_left)), [halo[12], None, halo[13]])
        right = plus(plus(halo[9:12], edge_left(to_right)), [None, halo[14], None])
        for k, plane in enumerate(interleaved(*lift(left, smooth, right))):
            c_ref[pl.ds(8 * k, 8), cut(t)] = plane
    i, j = (lax.broadcasted_iota(jnp.int32, (LANES, 2 * LANES), axis) for axis in (0, 1))
    spread = jnp.where(j == 2 * i, 1.0, 0.0).astype(jnp.bfloat16)
    even = (lane((6, LANES)) & 1) == 0
    split = parts(c_ref[...])
    for t in range(0, TILES, 2):
        wide = sum(
            jnp.dot(p[:, t * 64:t * 64 + LANES], spread, preferred_element_type=jnp.float32) for p in split
        )
        for half in (0, 1):
            for k in range(PAIRS):
                rows = rows_of(2 * k, 0, t + half)
                coarse = wide[8 * k:8 * k + 6, half * LANES:(half + 1) * LANES]
                o_ref[rows, :] = jnp.where(even, coarse, o_ref[rows, :])
    copies += [leave(x) for x in range(0, PLANES, 2)]
    for copy in copies:
        copy.wait()


VMEM = pl.BlockSpec(memory_space=pltpu.VMEM)
HBM = pl.BlockSpec(memory_space=pltpu.HBM)


def call(kernel, shapes, args, scratch=(), sems=0, out=VMEM, kind=jnp.float32, cost=None):
    return pl.pallas_call(
        kernel,
        out_shape=[jax.ShapeDtypeStruct(s, kind) for s in shapes],
        in_specs=[VMEM] * len(args),
        out_specs=[out] + [VMEM] * (len(shapes) - 1),
        scratch_shapes=[pltpu.VMEM(s, jnp.float32) for s in scratch] + [pltpu.SemaphoreType.DMA((sems,))] * (sems > 0),
        compiler_params=pltpu.CompilerParams(vmem_limit_bytes=16 << 20),
        cost_estimate=cost,
    )(*args)


def message(count):
    return (TILES * count, LANES)


def local(streams, spans, fields):
    def send(rows, target):
        pairs = [(s * spans + y, (lambda q: q[0] % streams * spans + q[1] % spans)(target(s, y))) for s in range(streams) for y in range(spans)]
        return lax.ppermute(rows, ("stream", "span"), pairs)

    cost = pl.CostEstimate(flops=10**9, bytes_accessed=10**6, transcendentals=0)
    fine, low = call(table_kernel, [(4 * LANES, 2 * LANES), (6 * LANES, 2 * LANES)], [], kind=jnp.bfloat16, cost=cost)
    block = (PLANES * ROWS * TILES, LANES)
    a, b, near, other, far = call(
        first_kernel,
        [(TILES, PLANES * ROWS, LANES), (TILES, PAIRS * ROWS, LANES), message(NEAR), message(EDGE), message(Y_FAR)],
        [fields.reshape(block), fine, low],
        [(PLANES * ROWS, CELLS // 2)],
    )
    near = send(near, lambda s, y: (s, y ^ 1))
    far = send(far, lambda s, y: (s, y + (2 if y % 2 else -2)))
    (other,) = call(fold_kernel, [message(EDGE)], [other, near])
    other = send(other, lambda s, y: (s, y + (1 if y % 2 else -1)))
    ya, yb, xnear, xother, xfar, xfar2 = call(
        middle_kernel,
        [(TILES, PLANES * 16, LANES), (TILES, PAIRS * 8, LANES), message(EDGE), message(EDGE), message(X_FAR), message(X_FAR)],
        [a, b, near, other, far, low],
        [(4, 96, LANES)],
    )
    xnear = send(xnear, lambda s, y: (s ^ 1, y))
    xother = send(xother, lambda s, y: (s + (1 if s % 2 else -1), y))
    xfar = send(xfar, lambda s, y: (s + (-2 if s // 2 % 2 else 2), y))
    xfar2 = send(xfar2, lambda s, y: (s + (2 if s // 2 % 2 else -2), y))
    (out,) = call(
        last_kernel,
        [block],
        [ya, yb, xnear, xother, xfar, xfar2],
        [(TILES, 96, LANES), (4, 120, LANES), (48, CELLS // 2), block],
        sems=PLANES,
        out=HBM,
    )
    return out.reshape(fields.shape)


def solution(mesh):
    return jax.shard_map(
        functools.partial(local, mesh.shape["stream"], mesh.shape["span"]),
        mesh=mesh,
        in_specs=(P(None, "stream", "span", None),),
        out_specs=P(None, "stream", "span", None),
        check_vma=False,
    )
```

```python
import functools

import jax
import jax.numpy as jnp
import ml_dtypes
import numpy as np
from jax import lax
from jax.experimental import pallas as pl
from jax.experimental.pallas import tpu as pltpu
from jax.sharding import PartitionSpec as P

NEAR_D, FAR_D = 0.5625, 0.0625
NEAR_S, FAR_S = 0.28125, 0.03125
PLANES, ROWS, CELLS, LANES = 12, 12, 1024, 128
TILES = CELLS // LANES
PAIRS = ROWS // 2


def total(a, b):
    return b if a is None else a if b is None else a + b


def scaled(factor, a):
    return None if a is None else factor * a


def near_far(near, far, a, b, c, d):
    return total(scaled(near, total(a, b)), scaled(far, total(c, d)))


def lift(left, cells, right):
    pairs = len(cells) // 2
    e = {i: cells[2 * i] for i in range(pairs)}
    o = {i: cells[2 * i + 1] for i in range(pairs)}
    if left is not None:
        o[-2], e[-1], o[-1] = left
    if right is not None:
        e[pairs], o[pairs], e[pairs + 1] = right
    d = {
        j: total(o.get(j), near_far(-NEAR_D, FAR_D, e.get(j), e.get(j + 1), e.get(j - 1), e.get(j + 2)))
        for j in range(-2, pairs + 1)
    }
    s = [
        total(e[i], near_far(NEAR_S, -FAR_S, d[i - 1], d[i], d[i - 2], d[i + 1]))
        for i in range(pairs)
    ]
    return s, [d[i] for i in range(pairs)]


def edge_right(c):
    return [
        total(c[-3], near_far(-NEAR_D, FAR_D, c[-4], None, c[-6], None)),
        c[-2],
        total(c[-1], scaled(FAR_D, c[-4])),
    ]


def edge_left(c):
    return [c[0], total(c[1], scaled(FAR_D, c[4])), c[2]]


def coarse_terms(c):
    zeros = [None] * len(c)
    to_right, _ = lift(edge_right(c), zeros, None)
    to_left, _ = lift(None, zeros, edge_left(c))
    return to_right, to_left


def plus(a, b):
    return [total(x, y) for x, y in zip(a, b)]


def interleaved(s, d):
    return [row for pair in zip(s, d) for row in pair]


def lane(shape):
    return lax.broadcasted_iota(jnp.int32, shape, len(shape) - 1)


def cut(t):
    return pl.ds(t * LANES, LANES)


def taps():
    v = np.eye(32)
    at = np.arange(32) % 2
    r = lambda k: np.roll(v, k, axis=1)
    v = np.where(at == 1, v - (NEAR_D * (r(1) + r(-1)) - FAR_D * (r(3) + r(-3))), v)
    v = np.where(at == 0, v + (NEAR_S * (r(1) + r(-1)) - FAR_S * (r(3) + r(-3))), v)
    assert (v == v.astype(ml_dtypes.bfloat16).astype(np.float64)).all()
    found = {k: (float(v[16 + k, 16]), float(v[17 + k, 17])) for k in range(-8, 9)}
    return {k: pair for k, pair in found.items() if any(pair)}


def table_kernel(fine_ref, low_ref):
    i, j = (lax.broadcasted_iota(jnp.int32, (LANES, LANES), axis) for axis in (0, 1))
    smooth = (j & 1) == 0
    value = {k: jnp.where(smooth, *pair) for k, pair in taps().items()}

    def block(step, tile):
        offset = i + tile * LANES - step * j
        out = jnp.zeros((LANES, LANES), jnp.float32)
        for k, v in value.items():
            out = jnp.where(offset == step * k, v, out)
        return out.astype(jnp.bfloat16)

    for ref, step in ((fine_ref, 1), (low_ref, 2)):
        ref[...] = jnp.zeros(ref.shape, jnp.bfloat16)
        for n in range(step + 2):
            one = block(step, n - 1)
            for column in (0, 1):
                ref[pl.ds((n + step * column) * LANES, LANES), cut(column)] = one


def parts(v):
    high = v.astype(jnp.bfloat16)
    rest = v - high.astype(jnp.float32)
    mid = rest.astype(jnp.bfloat16)
    return high, mid, (rest - mid.astype(jnp.float32)).astype(jnp.bfloat16)


def banded(tiles, m, starts, count):
    rows = tiles[0][0].shape[0]
    stacked = jnp.concatenate(
        [
            jnp.concatenate([tiles[(start + i) % TILES][part] for i in range(count)], axis=1)
            for part in range(3)
            for start in starts
        ],
        axis=0,
    )
    out = jnp.dot(stacked, m, preferred_element_type=jnp.float32)
    at_part = lambda part, n: out[(part * len(starts) + n) * rows:(part * len(starts) + n + 1) * rows]
    return [at_part(0, n) + (at_part(1, n) + at_part(2, n)) for n in range(len(starts))]


NEAR, EDGE, Y_FAR, X_FAR = 66, 54, 12, 6


def at(count, t, start, size):
    return pl.ds(t * count + start, size)


def span_edges(a_ref, b_ref, t):
    a = [a_ref[t, pl.ds(y, PLANES, stride=ROWS), :] for y in range(ROWS)]
    b = [b_ref[t, pl.ds(y, PAIRS, stride=ROWS), :] for y in range(ROWS)]
    return a, b


def put_rows(ref, start, rows, t):
    count = ref.shape[0] // TILES
    for row in rows:
        ref[at(count, t, start, row.shape[0]), :] = row
        start += row.shape[0]
    return start


def get_rows(ref, start, size, number, t):
    count = ref.shape[0] // TILES
    return [ref[at(count, t, start + size * j, size), :] for j in range(number)]


def choose(odd, a, b):
    return [jnp.where(odd, x, y) for x, y in zip(a, b)]


def first_kernel(f_ref, fine_ref, low_ref, a_ref, b_ref, near_ref, other_ref, far_ref, v_ref):
    odd_core = lax.axis_index("span") % 2 == 1
    tiles = [parts(f_ref[pl.ds(t, PLANES * ROWS, stride=TILES), :]) for t in range(TILES)]
    for q, block in enumerate([banded(tiles, fine_ref[...], (start,), 4)[0] for start in (-1, 1, 3, 5)]):
        for t in range(2):
            a_ref[2 * q + t] = block[:, t * LANES:(t + 1) * LANES]
    tiles = [parts(a_ref[t]) for t in range(TILES)]
    for q, block in enumerate([banded(tiles, low_ref[...], (start,), 6)[0] for start in (-1, 3)]):
        v_ref[:, pl.ds(256 * q, 256)] = block
    for t in range(TILES):
        for k in range(PAIRS):
            b_ref[t, pl.ds(k * ROWS, ROWS), :] = v_ref[pl.ds((2 * k + t // 4) * ROWS, ROWS), cut(t % 4)]
    for t in range(TILES):
        a, b = span_edges(a_ref, b_ref, t)
        smooth, _ = lift(None, b, None)
        to_right, to_left = coarse_terms(b)
        far_right, far_left = edge_right(to_right), edge_left(to_left)
        far_right, far_left = [far_right[0], far_right[2]], [far_left[1], jnp.zeros_like(far_left[1])]
        right = edge_right(a) + edge_right(smooth)
        left = edge_left(a) + edge_left(smooth)
        put_rows(near_ref, 0, choose(odd_core, left + far_left, right + far_right), t)
        put_rows(other_ref, 0, choose(odd_core, right, left), t)
        put_rows(far_ref, 0, choose(odd_core, far_right, far_left), t)


def fold_kernel(other_ref, near_ref, out_ref):
    odd_core = lax.axis_index("span") % 2 == 1
    out_ref[...] = other_ref[...]
    for t in range(TILES):
        one, two = get_rows(near_ref, EDGE, PAIRS, 2, t)
        zero = jnp.zeros_like(one)
        terms = choose(odd_core, [one, zero, two], [zero, one, zero])
        put_rows(out_ref, 36, plus(get_rows(other_ref, 36, PAIRS, 3, t), terms), t)


def low_rows(ref, low_ref, halo_ref):
    tiles = [parts(get_rows(ref, 0, 48, 1, t)[0]) for t in range(TILES)]
    for q, low in enumerate(banded(tiles, low_ref[...], (-1, 3), 6)):
        for t in range(2):
            halo_ref[2 * q + t] = low[:, t * LANES:(t + 1) * LANES]


def low_halo(halo_ref, t):
    return [halo_ref[t % 4, pl.ds(PLANES * j + t // 4, PAIRS, stride=2), :] for j in range(3)]


def one_side(odd, rows):
    zeros = [jnp.zeros_like(row) for row in rows]
    return choose(odd, rows, zeros), choose(odd, zeros, rows)


def near_kernel(a_ref, b_ref, near_ref, low_ref, ya_ref, s_ref, halo_ref):
    odd_core = lax.axis_index("span") % 2 == 1
    low_rows(near_ref, low_ref, halo_ref)
    for t in range(TILES):
        a, b = span_edges(a_ref, b_ref, t)
        left, right = one_side(odd_core, get_rows(near_ref, 0, PLANES, 3, t))
        smooth, detail = lift(left, a, right)
        for c in range(PAIRS):
            ya_ref[t, pl.ds(c, PLANES, stride=16), :] = smooth[c]
            ya_ref[t, pl.ds(8 + c, PLANES, stride=16), :] = detail[c]
        left, right = one_side(odd_core, low_halo(halo_ref, t))
        smooth, _ = lift(left, b, right)
        left, right = one_side(odd_core, get_rows(near_ref, 36, PAIRS, 3, t))
        to_right, to_left = coarse_terms(b)
        rows = smooth + plus(left, edge_right(to_left)) + plus(right, edge_left(to_right))
        for j, row in enumerate(rows):
            s_ref[t, pl.ds(8 * j, PAIRS), :] = row


def middle_kernel(near_ya_ref, s_ref, other_ref, far_ref, low_ref, ya_ref, yb_ref, xnear_ref, xother_ref, xfar_ref, xfar2_ref, halo_ref):
    odd_core = lax.axis_index("span") % 2 == 1
    odd_x = lax.axis_index("stream") % 2 == 1
    odd_pair = lax.axis_index("stream") // 2 % 2 == 1
    low_rows(other_ref, low_ref, halo_ref)
    for t in range(TILES):
        right, left = one_side(odd_core, get_rows(other_ref, 0, PLANES, 3, t))
        smooth, detail = lift(left, [None] * ROWS, right)
        for start, terms in ((0, smooth), (8, detail)):
            for c, term in enumerate(terms):
                rows = pl.ds(start + c, PLANES, stride=16)
                if term is not None:
                    ya_ref[t, rows, :] = near_ya_ref[t, rows, :] + term
                else:
                    ya_ref[t, rows, :] = near_ya_ref[t, rows, :]
        held = [s_ref[t, pl.ds(8 * j, PAIRS), :] for j in range(12)]
        right, left = one_side(odd_core, low_halo(halo_ref, t))
        terms, _ = lift(left, [None] * ROWS, right)
        smooth = plus(held[:6], terms)
        right, left = one_side(odd_core, get_rows(other_ref, 36, PAIRS, 3, t))
        one, two = get_rows(far_ref, 0, PAIRS, 2, t)
        zero = jnp.zeros_like(one)
        left = plus(plus(left, held[6:9]), choose(odd_core, [one, zero, two], [zero, zero, zero]))
        right = plus(plus(right, held[9:12]), choose(odd_core, [zero, zero, zero], [zero, one, zero]))
        smooth, detail = lift(left, smooth, right)
        for c, row in enumerate(interleaved(smooth, detail)):
            yb_ref[t, pl.ds(c, PAIRS, stride=8), :] = row
    for t in range(TILES):
        a = stream_planes(ya_ref, t)
        right, left = edge_right(a), edge_left(a)
        for ref, planes in ((xnear_ref, choose(odd_x, left, right)), (xother_ref, choose(odd_x, right, left))):
            put_rows(ref, 0, [half for plane in planes for half in (plane[0:6], plane[8:14])], t)
    for t in range(4):
        b = low_planes(yb_ref, t)
        smooth, _ = lift(None, b, None)
        to_right, to_left = coarse_terms(b)
        for half, planes in ((0, b), (4, smooth)):
            right, left = edge_right(planes), edge_left(planes)
            put_rows(xnear_ref, 36, [plane[0:6] for plane in choose(odd_x, left, right)], t + half)
            put_rows(xother_ref, 36, [plane[0:6] for plane in choose(odd_x, right, left)], t + half)
        far_right, far_left = edge_right(to_right), edge_left(to_left)
        far_right, far_left = [far_right[0], far_right[2]], [far_left[1], jnp.zeros_like(far_left[1])]
        for half in (0, 1):
            put_rows(xfar_ref, 0, [choose(odd_pair, far_left, far_right)[half][0:6]], t + 4 * half)
            put_rows(xfar2_ref, 0, [choose(odd_pair, far_right, far_left)[half][0:6]], t + 4 * half)


def stream_planes(ya_ref, t):
    return [ya_ref[t, pl.ds(16 * x, 16), :] for x in range(PLANES)]


def low_planes(yb_ref, t):
    return [yb_ref[t + 4 * odd, pl.ds(8 * k, 8), :] for k in range(PAIRS) for odd in (0, 1)]


def last_kernel(ya_ref, yb_ref, xnear_ref, xother_ref, xfar_ref, xfar2_ref, out_ref, la_ref, lb_ref, c_ref, o_ref, sems):
    odd_x = lax.axis_index("stream") % 2 == 1
    odd_pair = lax.axis_index("stream") // 2 % 2 == 1

    def rows_of(x, y, t):
        return pl.ds((x * ROWS + y) * TILES + t, PAIRS, stride=2 * TILES)

    def leave(x):
        rows = pl.ds(x * ROWS * TILES, ROWS * TILES)
        copy = pltpu.make_async_copy(o_ref.at[rows], out_ref.at[rows], sems.at[x])
        copy.start()
        return copy

    for t in range(TILES):
        near, other = (get_rows(ref, 0, 6, 6, t) for ref in (xnear_ref, xother_ref))
        for j, row in enumerate(choose(odd_x, near, other) + choose(odd_x, other, near)):
            la_ref[t, pl.ds(8 * j, 6), :] = row
        a = stream_planes(ya_ref, t)
        halo = [la_ref[t, pl.ds(16 * j, 16), :] for j in range(6)]
        for x, plane in enumerate(interleaved(*lift(halo[:3], a, halo[3:]))):
            o_ref[rows_of(x, 0, t), :] = plane[0:6]
            o_ref[rows_of(x, 1, t), :] = plane[8:14]
    copies = [leave(x) for x in range(1, PLANES, 2)]
    for t in range(4):
        b = low_planes(yb_ref, t)
        near, other = (get_rows(ref, 36, 6, 3, t) + get_rows(ref, 36, 6, 3, t + 4) for ref in (xnear_ref, xother_ref))
        far, far2 = (get_rows(ref, 0, 6, 1, t) + get_rows(ref, 0, 6, 1, t + 4) for ref in (xfar_ref, xfar2_ref))
        rows = choose(odd_x, near, other) + choose(odd_x, other, near)
        rows += choose(odd_pair, far, far2) + choose(odd_pair, far2, far)[:1]
        for j, row in enumerate(rows):
            lb_ref[t, pl.ds(8 * j, 6), :] = row
        halo = [lb_ref[t, pl.ds(8 * j, 8), :] for j in range(15)]
        smooth, _ = lift(halo[0:3], b, halo[6:9])
        to_right, to_left = coarse_terms(b)
        left = plus(plus(halo[3:6], edge_right(to_left)), [halo[12], None, halo[13]])
        right = plus(plus(halo[9:12], edge_left(to_right)), [None, halo[14], None])
        for k, plane in enumerate(interleaved(*lift(left, smooth, right))):
            c_ref[pl.ds(8 * k, 8), cut(t)] = plane
    i, j = (lax.broadcasted_iota(jnp.int32, (LANES, 2 * LANES), axis) for axis in (0, 1))
    spread = jnp.where(j == 2 * i, 1.0, 0.0).astype(jnp.bfloat16)
    even = (lane((6, LANES)) & 1) == 0
    split = parts(c_ref[...])
    for t in range(0, TILES, 2):
        wide = sum(
            jnp.dot(p[:, t * 64:t * 64 + LANES], spread, preferred_element_type=jnp.float32) for p in split
        )
        for half in (0, 1):
            for k in range(PAIRS):
                rows = rows_of(2 * k, 0, t + half)
                coarse = wide[8 * k:8 * k + 6, half * LANES:(half + 1) * LANES]
                o_ref[rows, :] = jnp.where(even, coarse, o_ref[rows, :])
    copies += [leave(x) for x in range(0, PLANES, 2)]
    for copy in copies:
        copy.wait()


VMEM = pl.BlockSpec(memory_space=pltpu.VMEM)
HBM = pl.BlockSpec(memory_space=pltpu.HBM)


def call(kernel, shapes, args, scratch=(), sems=0, out=VMEM, kind=jnp.float32, cost=None):
    return pl.pallas_call(
        kernel,
        out_shape=[jax.ShapeDtypeStruct(s, kind) for s in shapes],
        in_specs=[VMEM] * len(args),
        out_specs=[out] + [VMEM] * (len(shapes) - 1),
        scratch_shapes=[pltpu.VMEM(s, jnp.float32) for s in scratch] + [pltpu.SemaphoreType.DMA((sems,))] * (sems > 0),
        compiler_params=pltpu.CompilerParams(vmem_limit_bytes=16 << 20),
        cost_estimate=cost,
    )(*args)


def message(count):
    return (TILES * count, LANES)


def local(streams, spans, fields):
    def send(rows, target):
        pairs = [(s * spans + y, (lambda q: q[0] % streams * spans + q[1] % spans)(target(s, y))) for s in range(streams) for y in range(spans)]
        return lax.ppermute(rows, ("stream", "span"), pairs)

    cost = pl.CostEstimate(flops=10**9, bytes_accessed=10**6, transcendentals=0)
    fine, low = call(table_kernel, [(4 * LANES, 2 * LANES), (6 * LANES, 2 * LANES)], [], kind=jnp.bfloat16, cost=cost)
    block = (PLANES * ROWS * TILES, LANES)
    a, b, near, other, far = call(
        first_kernel,
        [(TILES, PLANES * ROWS, LANES), (TILES, PAIRS * ROWS, LANES), message(NEAR), message(EDGE), message(Y_FAR)],
        [fields.reshape(block), fine, low],
        [(PLANES * ROWS, CELLS // 2)],
    )
    near = send(near, lambda s, y: (s, y ^ 1))
    far = send(far, lambda s, y: (s, y + (2 if y % 2 else -2)))
    (other,) = call(fold_kernel, [message(EDGE)], [other, near])
    other = send(other, lambda s, y: (s, y + (1 if y % 2 else -1)))
    ya, smooth = call(
        near_kernel,
        [(TILES, PLANES * 16, LANES), (TILES, 96, LANES)],
        [a, b, near, low],
        [(4, 48, LANES)],
        cost=cost,
    )
    ya, yb, xnear, xother, xfar, xfar2 = call(
        middle_kernel,
        [(TILES, PLANES * 16, LANES), (TILES, PAIRS * 8, LANES), message(EDGE), message(EDGE), message(X_FAR), message(X_FAR)],
        [ya, smooth, other, far, low],
        [(4, 48, LANES)],
    )
    xnear = send(xnear, lambda s, y: (s ^ 1, y))
    xother = send(xother, lambda s, y: (s + (1 if s % 2 else -1), y))
    xfar = send(xfar, lambda s, y: (s + (-2 if s // 2 % 2 else 2), y))
    xfar2 = send(xfar2, lambda s, y: (s + (2 if s // 2 % 2 else -2), y))
    (out,) = call(
        last_kernel,
        [block],
        [ya, yb, xnear, xother, xfar, xfar2],
        [(TILES, 96, LANES), (4, 120, LANES), (48, CELLS // 2), block],
        sems=PLANES,
        out=HBM,
    )
    return out.reshape(fields.shape)


def solution(mesh):
    return jax.shard_map(
        functools.partial(local, mesh.shape["stream"], mesh.shape["span"]),
        mesh=mesh,
        in_specs=(P(None, "stream", "span", None),),
        out_specs=P(None, "stream", "span", None),
        check_vma=False,
    )
```

```python
import functools

import jax
import jax.numpy as jnp
import ml_dtypes
import numpy as np
from jax import lax
from jax.experimental import pallas as pl
from jax.experimental.pallas import tpu as pltpu
from jax.sharding import PartitionSpec as P

NEAR_D, FAR_D = 0.5625, 0.0625
NEAR_S, FAR_S = 0.28125, 0.03125
PLANES, ROWS, CELLS, LANES = 12, 12, 1024, 128
TILES = CELLS // LANES
PAIRS = ROWS // 2


def total(a, b):
    return b if a is None else a if b is None else a + b


def scaled(factor, a):
    return None if a is None else factor * a


def near_far(near, far, a, b, c, d):
    return total(scaled(near, total(a, b)), scaled(far, total(c, d)))


def lift(left, cells, right):
    pairs = len(cells) // 2
    e = {i: cells[2 * i] for i in range(pairs)}
    o = {i: cells[2 * i + 1] for i in range(pairs)}
    if left is not None:
        o[-2], e[-1], o[-1] = left
    if right is not None:
        e[pairs], o[pairs], e[pairs + 1] = right
    d = {
        j: total(o.get(j), near_far(-NEAR_D, FAR_D, e.get(j), e.get(j + 1), e.get(j - 1), e.get(j + 2)))
        for j in range(-2, pairs + 1)
    }
    s = [
        total(e[i], near_far(NEAR_S, -FAR_S, d[i - 1], d[i], d[i - 2], d[i + 1]))
        for i in range(pairs)
    ]
    return s, [d[i] for i in range(pairs)]


def edge_right(c):
    return [
        total(c[-3], near_far(-NEAR_D, FAR_D, c[-4], None, c[-6], None)),
        c[-2],
        total(c[-1], scaled(FAR_D, c[-4])),
    ]


def edge_left(c):
    return [c[0], total(c[1], scaled(FAR_D, c[4])), c[2]]


def coarse_terms(c):
    zeros = [None] * len(c)
    to_right, _ = lift(edge_right(c), zeros, None)
    to_left, _ = lift(None, zeros, edge_left(c))
    return to_right, to_left


def plus(a, b):
    return [total(x, y) for x, y in zip(a, b)]


def interleaved(s, d):
    return [row for pair in zip(s, d) for row in pair]


def lane(shape):
    return lax.broadcasted_iota(jnp.int32, shape, len(shape) - 1)


def cut(t):
    return pl.ds(t * LANES, LANES)


def taps():
    v = np.eye(32)
    at = np.arange(32) % 2
    r = lambda k: np.roll(v, k, axis=1)
    v = np.where(at == 1, v - (NEAR_D * (r(1) + r(-1)) - FAR_D * (r(3) + r(-3))), v)
    v = np.where(at == 0, v + (NEAR_S * (r(1) + r(-1)) - FAR_S * (r(3) + r(-3))), v)
    assert (v == v.astype(ml_dtypes.bfloat16).astype(np.float64)).all()
    found = {k: (float(v[16 + k, 16]), float(v[17 + k, 17])) for k in range(-8, 9)}
    return {k: pair for k, pair in found.items() if any(pair)}


def table_kernel(fine_ref, low_ref):
    i, j = (lax.broadcasted_iota(jnp.int32, (LANES, LANES), axis) for axis in (0, 1))
    smooth = (j & 1) == 0
    value = {k: jnp.where(smooth, *pair) for k, pair in taps().items()}

    def block(step, tile):
        offset = i + tile * LANES - step * j
        out = jnp.zeros((LANES, LANES), jnp.float32)
        for k, v in value.items():
            out = jnp.where(offset == step * k, v, out)
        return out.astype(jnp.bfloat16)

    for ref, step in ((fine_ref, 1), (low_ref, 2)):
        ref[...] = jnp.zeros(ref.shape, jnp.bfloat16)
        for n in range(step + 2):
            one = block(step, n - 1)
            for column in (0, 1):
                ref[pl.ds((n + step * column) * LANES, LANES), cut(column)] = one


def parts(v):
    high = v.astype(jnp.bfloat16)
    rest = v - high.astype(jnp.float32)
    mid = rest.astype(jnp.bfloat16)
    return high, mid, (rest - mid.astype(jnp.float32)).astype(jnp.bfloat16)


def banded(tiles, m, starts, count):
    rows = tiles[0][0].shape[0]
    stacked = jnp.concatenate(
        [
            jnp.concatenate([tiles[(start + i) % TILES][part] for i in range(count)], axis=1)
            for part in range(3)
            for start in starts
        ],
        axis=0,
    )
    out = jnp.dot(stacked, m, preferred_element_type=jnp.float32)
    at_part = lambda part, n: out[(part * len(starts) + n) * rows:(part * len(starts) + n + 1) * rows]
    return [at_part(0, n) + (at_part(1, n) + at_part(2, n)) for n in range(len(starts))]


NEAR, EDGE, Y_FAR, X_FAR = 66, 54, 12, 6


def at(count, t, start, size):
    return pl.ds(t * count + start, size)


def span_edges(a_ref, b_ref, t):
    a = [a_ref[t, pl.ds(y, PLANES, stride=ROWS), :] for y in range(ROWS)]
    b = [b_ref[t, pl.ds(y, PAIRS, stride=ROWS), :] for y in range(ROWS)]
    return a, b


def put_rows(ref, start, rows, t):
    count = ref.shape[0] // TILES
    for row in rows:
        ref[at(count, t, start, row.shape[0]), :] = row
        start += row.shape[0]
    return start


def get_rows(ref, start, size, number, t):
    count = ref.shape[0] // TILES
    return [ref[at(count, t, start + size * j, size), :] for j in range(number)]


def choose(odd, a, b):
    return [jnp.where(odd, x, y) for x, y in zip(a, b)]


def first_kernel(f_ref, fine_ref, low_ref, a_ref, b_ref, near_ref, other_ref, far_ref, v_ref):
    odd_core = lax.axis_index("span") % 2 == 1
    tiles = [parts(f_ref[pl.ds(t, PLANES * ROWS, stride=TILES), :]) for t in range(TILES)]
    for q, block in enumerate([banded(tiles, fine_ref[...], (start,), 4)[0] for start in (-1, 1, 3, 5)]):
        for t in range(2):
            a_ref[2 * q + t] = block[:, t * LANES:(t + 1) * LANES]
    tiles = [parts(a_ref[t]) for t in range(TILES)]
    for q, block in enumerate([banded(tiles, low_ref[...], (start,), 6)[0] for start in (-1, 3)]):
        v_ref[:, pl.ds(256 * q, 256)] = block
    for t in range(TILES):
        for k in range(PAIRS):
            b_ref[t, pl.ds(k * ROWS, ROWS), :] = v_ref[pl.ds((2 * k + t // 4) * ROWS, ROWS), cut(t % 4)]
    for t in range(TILES):
        a, b = span_edges(a_ref, b_ref, t)
        smooth, _ = lift(None, b, None)
        to_right, to_left = coarse_terms(b)
        far_right, far_left = edge_right(to_right), edge_left(to_left)
        far_right, far_left = [far_right[0], far_right[2]], [far_left[1], jnp.zeros_like(far_left[1])]
        right = edge_right(a) + edge_right(smooth)
        left = edge_left(a) + edge_left(smooth)
        put_rows(near_ref, 0, choose(odd_core, left + far_left, right + far_right), t)
        put_rows(other_ref, 0, choose(odd_core, right, left), t)
        put_rows(far_ref, 0, choose(odd_core, far_right, far_left), t)


def fold_kernel(other_ref, near_ref, out_ref):
    odd_core = lax.axis_index("span") % 2 == 1
    out_ref[...] = other_ref[...]
    for t in range(TILES):
        one, two = get_rows(near_ref, EDGE, PAIRS, 2, t)
        zero = jnp.zeros_like(one)
        terms = choose(odd_core, [one, zero, two], [zero, one, zero])
        put_rows(out_ref, 36, plus(get_rows(other_ref, 36, PAIRS, 3, t), terms), t)


def low_rows(ref, low_ref, halo_ref):
    tiles = [parts(get_rows(ref, 0, 48, 1, t)[0]) for t in range(TILES)]
    for q, low in enumerate(banded(tiles, low_ref[...], (-1, 3), 6)):
        for t in range(2):
            halo_ref[2 * q + t] = low[:, t * LANES:(t + 1) * LANES]


def low_halo(halo_ref, t):
    return [halo_ref[t % 4, pl.ds(PLANES * j + t // 4, PAIRS, stride=2), :] for j in range(3)]


def one_side(odd, rows):
    zeros = [jnp.zeros_like(row) for row in rows]
    return choose(odd, rows, zeros), choose(odd, zeros, rows)


def near_kernel(a_ref, b_ref, near_ref, low_ref, ya_ref, s_ref, halo_ref):
    odd_core = lax.axis_index("span") % 2 == 1
    low_rows(near_ref, low_ref, halo_ref)
    for t in range(TILES):
        a, b = span_edges(a_ref, b_ref, t)
        left, right = one_side(odd_core, get_rows(near_ref, 0, PLANES, 3, t))
        smooth, detail = lift(left, a, right)
        for c in range(PAIRS):
            ya_ref[t, pl.ds(c, PLANES, stride=16), :] = smooth[c]
            ya_ref[t, pl.ds(8 + c, PLANES, stride=16), :] = detail[c]
        left, right = one_side(odd_core, low_halo(halo_ref, t))
        smooth, _ = lift(left, b, right)
        left, right = one_side(odd_core, get_rows(near_ref, 36, PAIRS, 3, t))
        to_right, to_left = coarse_terms(b)
        rows = smooth + plus(left, edge_right(to_left)) + plus(right, edge_left(to_right))
        for j, row in enumerate(rows):
            s_ref[t, pl.ds(8 * j, PAIRS), :] = row


def middle_kernel(near_ya_ref, s_ref, other_ref, far_ref, low_ref, ya_ref, yb_ref, xnear_ref, xother_ref, xfar_ref, xfar2_ref, halo_ref):
    odd_core = lax.axis_index("span") % 2 == 1
    odd_x = lax.axis_index("stream") % 2 == 1
    odd_pair = lax.axis_index("stream") // 2 % 2 == 1
    low_rows(other_ref, low_ref, halo_ref)
    for t in range(TILES):
        right, left = one_side(odd_core, get_rows(other_ref, 0, PLANES, 3, t))
        smooth, detail = lift(left, [None] * ROWS, right)
        for start, terms in ((0, smooth), (8, detail)):
            for c, term in enumerate(terms):
                rows = pl.ds(start + c, PLANES, stride=16)
                if term is not None:
                    ya_ref[t, rows, :] = near_ya_ref[t, rows, :] + term
                else:
                    ya_ref[t, rows, :] = near_ya_ref[t, rows, :]
        held = [s_ref[t, pl.ds(8 * j, PAIRS), :] for j in range(12)]
        right, left = one_side(odd_core, low_halo(halo_ref, t))
        terms, _ = lift(left, [None] * ROWS, right)
        smooth = plus(held[:6], terms)
        right, left = one_side(odd_core, get_rows(other_ref, 36, PAIRS, 3, t))
        one, two = get_rows(far_ref, 0, PAIRS, 2, t)
        zero = jnp.zeros_like(one)
        left = plus(plus(left, held[6:9]), choose(odd_core, [one, zero, two], [zero, zero, zero]))
        right = plus(plus(right, held[9:12]), choose(odd_core, [zero, zero, zero], [zero, one, zero]))
        smooth, detail = lift(left, smooth, right)
        for c, row in enumerate(interleaved(smooth, detail)):
            yb_ref[t, pl.ds(c, PAIRS, stride=8), :] = row
    for t in range(TILES):
        a = stream_planes(ya_ref, t)
        right, left = edge_right(a), edge_left(a)
        for ref, planes in ((xnear_ref, choose(odd_x, left, right)), (xother_ref, choose(odd_x, right, left))):
            put_rows(ref, 0, [half for plane in planes for half in (plane[0:6], plane[8:14])], t)
    for t in range(4):
        b = low_planes(yb_ref, t)
        smooth, _ = lift(None, b, None)
        to_right, to_left = coarse_terms(b)
        for half, planes in ((0, b), (4, smooth)):
            right, left = edge_right(planes), edge_left(planes)
            put_rows(xnear_ref, 36, [plane[0:6] for plane in choose(odd_x, left, right)], t + half)
            put_rows(xother_ref, 36, [plane[0:6] for plane in choose(odd_x, right, left)], t + half)
        far_right, far_left = edge_right(to_right), edge_left(to_left)
        far_right, far_left = [far_right[0], far_right[2]], [far_left[1], jnp.zeros_like(far_left[1])]
        for half in (0, 1):
            put_rows(xfar_ref, 0, [choose(odd_pair, far_left, far_right)[half][0:6]], t + 4 * half)
            put_rows(xfar2_ref, 0, [choose(odd_pair, far_right, far_left)[half][0:6]], t + 4 * half)


def stream_planes(ya_ref, t):
    return [ya_ref[t, pl.ds(16 * x, 16), :] for x in range(PLANES)]


def low_planes(yb_ref, t):
    return [yb_ref[t + 4 * odd, pl.ds(8 * k, 8), :] for k in range(PAIRS) for odd in (0, 1)]


def rows_of(x, y, t):
    return pl.ds((x * ROWS + y) * TILES + t, PAIRS, stride=2 * TILES)


def own_kernel(ya_ref, yb_ref, part_ref, s_ref):
    for t in range(TILES):
        for x, plane in enumerate(interleaved(*lift(None, stream_planes(ya_ref, t), None))):
            part_ref[rows_of(x, 0, t), :] = plane[0:6]
            part_ref[rows_of(x, 1, t), :] = plane[8:14]
    for t in range(4):
        b = low_planes(yb_ref, t)
        smooth, _ = lift(None, b, None)
        to_right, to_left = coarse_terms(b)
        for j, row in enumerate(smooth + edge_right(to_left) + edge_left(to_right)):
            s_ref[t, pl.ds(8 * j, 8), :] = row


def last_kernel(part_ref, s_ref, xnear_ref, xother_ref, xfar_ref, xfar2_ref, out_ref, c_ref, o_ref, sems):
    odd_x = lax.axis_index("stream") % 2 == 1
    odd_pair = lax.axis_index("stream") // 2 % 2 == 1

    def leave(ref, x):
        rows = pl.ds(x * ROWS * TILES, ROWS * TILES)
        copy = pltpu.make_async_copy(ref.at[rows], out_ref.at[rows], sems.at[x])
        copy.start()
        return copy

    apart = (3, 5, 7)
    copies = [leave(part_ref, x) for x in apart]
    for t in range(TILES):
        near, other = (get_rows(ref, 0, 6, 6, t) for ref in (xnear_ref, xother_ref))
        left, right = choose(odd_x, near, other), choose(odd_x, other, near)
        for y in (0, 1):
            terms = interleaved(*lift(left[y::2], [None] * PLANES, right[y::2]))
            for x, term in enumerate(terms):
                if x not in apart:
                    rows = rows_of(x, y, t)
                    o_ref[rows, :] = total(part_ref[rows, :], term)
    copies += [leave(o_ref, x) for x in range(1, PLANES, 2) if x not in apart]
    for t in range(4):
        near, other = (get_rows(ref, 36, 6, 3, t) + get_rows(ref, 36, 6, 3, t + 4) for ref in (xnear_ref, xother_ref))
        far, far2 = (get_rows(ref, 0, 6, 1, t) + get_rows(ref, 0, 6, 1, t + 4) for ref in (xfar_ref, xfar2_ref))
        left, right = choose(odd_x, near, other), choose(odd_x, other, near)
        far_left, far_right = choose(odd_pair, far, far2), choose(odd_pair, far2, far)
        held = [s_ref[t, pl.ds(8 * j, 6), :] for j in range(12)]
        terms, _ = lift(left[:3], [None] * PLANES, right[:3])
        smooth = plus(held[:6], terms)
        left = plus(plus(left[3:], held[6:9]), [far_left[0], None, far_left[1]])
        right = plus(plus(right[3:], held[9:12]), [None, far_right[0], None])
        for k, plane in enumerate(interleaved(*lift(left, smooth, right))):
            c_ref[pl.ds(8 * k, 6), cut(t)] = plane
    i, j = (lax.broadcasted_iota(jnp.int32, (LANES, 2 * LANES), axis) for axis in (0, 1))
    spread = jnp.where(j == 2 * i, 1.0, 0.0).astype(jnp.bfloat16)
    even = (lane((6, LANES)) & 1) == 0
    split = parts(c_ref[...])
    for t in range(0, TILES, 2):
        wide = sum(
            jnp.dot(p[:, t * 64:t * 64 + LANES], spread, preferred_element_type=jnp.float32) for p in split
        )
        for half in (0, 1):
            for k in range(PAIRS):
                rows = rows_of(2 * k, 0, t + half)
                coarse = wide[8 * k:8 * k + 6, half * LANES:(half + 1) * LANES]
                o_ref[rows, :] = jnp.where(even, coarse, o_ref[rows, :])
    copies += [leave(o_ref, x) for x in range(0, PLANES, 2)]
    for copy in copies:
        copy.wait()


VMEM = pl.BlockSpec(memory_space=pltpu.VMEM)
HBM = pl.BlockSpec(memory_space=pltpu.HBM)


def call(kernel, shapes, args, scratch=(), sems=0, out=VMEM, kind=jnp.float32, cost=None):
    return pl.pallas_call(
        kernel,
        out_shape=[jax.ShapeDtypeStruct(s, kind) for s in shapes],
        in_specs=[VMEM] * len(args),
        out_specs=[out] + [VMEM] * (len(shapes) - 1),
        scratch_shapes=[pltpu.VMEM(s, jnp.float32) for s in scratch] + [pltpu.SemaphoreType.DMA((sems,))] * (sems > 0),
        compiler_params=pltpu.CompilerParams(vmem_limit_bytes=16 << 20),
        cost_estimate=cost,
    )(*args)


def message(count):
    return (TILES * count, LANES)


def local(streams, spans, fields):
    def send(rows, target):
        pairs = [(s * spans + y, (lambda q: q[0] % streams * spans + q[1] % spans)(target(s, y))) for s in range(streams) for y in range(spans)]
        return lax.ppermute(rows, ("stream", "span"), pairs)

    cost = pl.CostEstimate(flops=10**9, bytes_accessed=10**6, transcendentals=0)
    fine, low = call(table_kernel, [(4 * LANES, 2 * LANES), (6 * LANES, 2 * LANES)], [], kind=jnp.bfloat16, cost=cost)
    block = (PLANES * ROWS * TILES, LANES)
    a, b, near, other, far = call(
        first_kernel,
        [(TILES, PLANES * ROWS, LANES), (TILES, PAIRS * ROWS, LANES), message(NEAR), message(EDGE), message(Y_FAR)],
        [fields.reshape(block), fine, low],
        [(PLANES * ROWS, CELLS // 2)],
    )
    near = send(near, lambda s, y: (s, y ^ 1))
    far = send(far, lambda s, y: (s, y + (2 if y % 2 else -2)))
    (other,) = call(fold_kernel, [message(EDGE)], [other, near])
    other = send(other, lambda s, y: (s, y + (1 if y % 2 else -1)))
    ya, smooth = call(
        near_kernel,
        [(TILES, PLANES * 16, LANES), (TILES, 96, LANES)],
        [a, b, near, low],
        [(4, 48, LANES)],
        cost=cost,
    )
    ya, yb, xnear, xother, xfar, xfar2 = call(
        middle_kernel,
        [(TILES, PLANES * 16, LANES), (TILES, PAIRS * 8, LANES), message(EDGE), message(EDGE), message(X_FAR), message(X_FAR)],
        [ya, smooth, other, far, low],
        [(4, 48, LANES)],
    )
    xnear = send(xnear, lambda s, y: (s ^ 1, y))
    xother = send(xother, lambda s, y: (s + (1 if s % 2 else -1), y))
    xfar = send(xfar, lambda s, y: (s + (-2 if s // 2 % 2 else 2), y))
    xfar2 = send(xfar2, lambda s, y: (s + (2 if s // 2 % 2 else -2), y))
    part, smooth = call(own_kernel, [block, (4, 96, LANES)], [ya, yb], cost=cost)
    (out,) = call(
        last_kernel,
        [block],
        [part, smooth, xnear, xother, xfar, xfar2],
        [(48, CELLS // 2), block],
        sems=PLANES,
        out=HBM,
    )
    return out.reshape(fields.shape)


def solution(mesh):
    return jax.shard_map(
        functools.partial(local, mesh.shape["stream"], mesh.shape["span"]),
        mesh=mesh,
        in_specs=(P(None, "stream", "span", None),),
        out_specs=P(None, "stream", "span", None),
        check_vma=False,
    )
```

```python
import functools

import jax
import jax.numpy as jnp
import ml_dtypes
import numpy as np
from jax import lax
from jax.experimental import pallas as pl
from jax.experimental.pallas import tpu as pltpu
from jax.sharding import PartitionSpec as P

NEAR_D, FAR_D = 0.5625, 0.0625
NEAR_S, FAR_S = 0.28125, 0.03125
PLANES, ROWS, CELLS, LANES = 12, 12, 1024, 128
TILES = CELLS // LANES
PAIRS = ROWS // 2


def total(a, b):
    return b if a is None else a if b is None else a + b


def scaled(factor, a):
    return None if a is None else factor * a


def near_far(near, far, a, b, c, d):
    return total(scaled(near, total(a, b)), scaled(far, total(c, d)))


def lift(left, cells, right):
    pairs = len(cells) // 2
    e = {i: cells[2 * i] for i in range(pairs)}
    o = {i: cells[2 * i + 1] for i in range(pairs)}
    if left is not None:
        o[-2], e[-1], o[-1] = left
    if right is not None:
        e[pairs], o[pairs], e[pairs + 1] = right
    d = {
        j: total(o.get(j), near_far(-NEAR_D, FAR_D, e.get(j), e.get(j + 1), e.get(j - 1), e.get(j + 2)))
        for j in range(-2, pairs + 1)
    }
    s = [
        total(e[i], near_far(NEAR_S, -FAR_S, d[i - 1], d[i], d[i - 2], d[i + 1]))
        for i in range(pairs)
    ]
    return s, [d[i] for i in range(pairs)]


def edge_right(c):
    return [
        total(c[-3], near_far(-NEAR_D, FAR_D, c[-4], None, c[-6], None)),
        c[-2],
        total(c[-1], scaled(FAR_D, c[-4])),
    ]


def edge_left(c):
    return [c[0], total(c[1], scaled(FAR_D, c[4])), c[2]]


def coarse_terms(c):
    zeros = [None] * len(c)
    to_right, _ = lift(edge_right(c), zeros, None)
    to_left, _ = lift(None, zeros, edge_left(c))
    return to_right, to_left


def plus(a, b):
    return [total(x, y) for x, y in zip(a, b)]


def interleaved(s, d):
    return [row for pair in zip(s, d) for row in pair]


def lane(shape):
    return lax.broadcasted_iota(jnp.int32, shape, len(shape) - 1)


def cut(t):
    return pl.ds(t * LANES, LANES)


def taps():
    v = np.eye(32)
    at = np.arange(32) % 2
    r = lambda k: np.roll(v, k, axis=1)
    v = np.where(at == 1, v - (NEAR_D * (r(1) + r(-1)) - FAR_D * (r(3) + r(-3))), v)
    v = np.where(at == 0, v + (NEAR_S * (r(1) + r(-1)) - FAR_S * (r(3) + r(-3))), v)
    assert (v == v.astype(ml_dtypes.bfloat16).astype(np.float64)).all()
    found = {k: (float(v[16 + k, 16]), float(v[17 + k, 17])) for k in range(-8, 9)}
    return {k: pair for k, pair in found.items() if any(pair)}


def table_kernel(fine_ref, low_ref):
    i, j = (lax.broadcasted_iota(jnp.int32, (LANES, LANES), axis) for axis in (0, 1))
    smooth = (j & 1) == 0
    value = {k: jnp.where(smooth, *pair) for k, pair in taps().items()}

    def block(step, tile):
        offset = i + tile * LANES - step * j
        out = jnp.zeros((LANES, LANES), jnp.float32)
        for k, v in value.items():
            out = jnp.where(offset == step * k, v, out)
        return out.astype(jnp.bfloat16)

    for ref, step in ((fine_ref, 1), (low_ref, 2)):
        ref[...] = jnp.zeros(ref.shape, jnp.bfloat16)
        for n in range(step + 2):
            one = block(step, n - 1)
            for column in (0, 1):
                ref[pl.ds((n + step * column) * LANES, LANES), cut(column)] = one


def parts(v):
    high = v.astype(jnp.bfloat16)
    rest = v - high.astype(jnp.float32)
    mid = rest.astype(jnp.bfloat16)
    return high, mid, (rest - mid.astype(jnp.float32)).astype(jnp.bfloat16)


def banded(tiles, m, starts, count):
    rows = tiles[0][0].shape[0]
    stacked = jnp.concatenate(
        [
            jnp.concatenate([tiles[(start + i) % TILES][part] for i in range(count)], axis=1)
            for part in range(3)
            for start in starts
        ],
        axis=0,
    )
    out = jnp.dot(stacked, m, preferred_element_type=jnp.float32)
    at_part = lambda part, n: out[(part * len(starts) + n) * rows:(part * len(starts) + n + 1) * rows]
    return [at_part(0, n) + (at_part(1, n) + at_part(2, n)) for n in range(len(starts))]


EDGE, Y_FAR, X_FAR = 54, 12, 6
FIRST, SECOND = (0, 1, 2, 6, 8, 9, 10, 11), (3, 4, 5, 7)


def at(count, t, start, size):
    return pl.ds(t * count + start, size)


def fine_rows(refs, t):
    found = {y: ref[t, pl.ds(PLANES * n, PLANES), :] for ref, ys in refs for n, y in enumerate(ys)}
    return [found.get(y) for y in range(ROWS)]


def deep_rows(refs, t):
    found = {
        y: ref[t % 4, pl.ds(PLANES * n + t // 4, PAIRS, stride=2), :] for ref, ys in refs for n, y in enumerate(ys)
    }
    return [found.get(y) for y in range(ROWS)]


def put_rows(ref, start, rows, t):
    count = ref.shape[0] // TILES
    for row in rows:
        ref[at(count, t, start, row.shape[0]), :] = row
        start += row.shape[0]
    return start


def get_rows(ref, start, size, number, t):
    count = ref.shape[0] // TILES
    return [ref[at(count, t, start + size * j, size), :] for j in range(number)]


def choose(odd, a, b):
    return [jnp.where(odd, x, y) for x, y in zip(a, b)]


def lift_cells(f_ref, fine_ref, low_ref, ys, a_ref, b_ref):
    for t in range(TILES):
        for n, y in enumerate(ys):
            a_ref[t, pl.ds(PLANES * n, PLANES), :] = f_ref[pl.ds(y * TILES + t, PLANES, stride=ROWS * TILES), :]
    tiles = [parts(a_ref[t]) for t in range(TILES)]
    for q, start in enumerate((-1, 1, 3, 5)):
        (block,) = banded(tiles, fine_ref[...], (start,), 4)
        for t in range(2):
            a_ref[2 * q + t] = block[:, t * LANES:(t + 1) * LANES]
    tiles = [parts(a_ref[t]) for t in range(TILES)]
    for q, start in enumerate((-1, 3)):
        (block,) = banded(tiles, low_ref[...], (start,), 6)
        for t in range(2):
            b_ref[2 * q + t] = block[:, t * LANES:(t + 1) * LANES]


def first_kernel(f_ref, fine_ref, low_ref, a_ref, b_ref, behind_ref, far_ref):
    odd_core = lax.axis_index("span") % 2 == 1
    lift_cells(f_ref, fine_ref, low_ref, FIRST, a_ref, b_ref)
    for t in range(TILES):
        to_right, to_left = coarse_terms(deep_rows([(b_ref, FIRST)], t))
        far_right, far_left = edge_right(to_right), edge_left(to_left)
        far_right, far_left = [far_right[0], far_right[2]], [far_left[1], jnp.zeros_like(far_left[1])]
        put_rows(behind_ref, 0, choose(odd_core, far_left, far_right), t)
        put_rows(far_ref, 0, choose(odd_core, far_right, far_left), t)


def second_kernel(f_ref, fine_ref, low_ref, a_ref, b_ref, a2_ref, b2_ref, near_ref, other_ref):
    odd_core = lax.axis_index("span") % 2 == 1
    lift_cells(f_ref, fine_ref, low_ref, SECOND, a2_ref, b2_ref)
    for t in range(TILES):
        a = fine_rows([(a_ref, FIRST), (a2_ref, SECOND)], t)
        smooth, _ = lift(None, deep_rows([(b_ref, FIRST), (b2_ref, SECOND)], t), None)
        right = edge_right(a) + edge_right(smooth)
        left = edge_left(a) + edge_left(smooth)
        put_rows(near_ref, 0, choose(odd_core, left, right), t)
        put_rows(other_ref, 0, choose(odd_core, right, left), t)


def fold_kernel(other_ref, behind_ref, near_ref, out_ref, near_out_ref):
    odd_core = lax.axis_index("span") % 2 == 1
    out_ref[...] = other_ref[...]
    near_out_ref[...] = near_ref[...]
    for t in range(TILES):
        one, two = get_rows(behind_ref, 0, PAIRS, 2, t)
        zero = jnp.zeros_like(one)
        terms = choose(odd_core, [one, zero, two], [zero, one, zero])
        put_rows(out_ref, 36, plus(get_rows(other_ref, 36, PAIRS, 3, t), terms), t)


def low_rows(ref, low_ref, halo_ref):
    tiles = [parts(get_rows(ref, 0, 48, 1, t)[0]) for t in range(TILES)]
    for q, low in enumerate(banded(tiles, low_ref[...], (-1, 3), 6)):
        for t in range(2):
            halo_ref[2 * q + t] = low[:, t * LANES:(t + 1) * LANES]


def low_halo(halo_ref, t):
    return [halo_ref[t % 4, pl.ds(PLANES * j + t // 4, PAIRS, stride=2), :] for j in range(3)]


def one_side(odd, rows):
    zeros = [jnp.zeros_like(row) for row in rows]
    return choose(odd, rows, zeros), choose(odd, zeros, rows)


def near_kernel(a_ref, b_ref, a2_ref, b2_ref, near_ref, low_ref, ya_ref, s_ref, halo_ref):
    odd_core = lax.axis_index("span") % 2 == 1
    low_rows(near_ref, low_ref, halo_ref)
    for t in range(TILES):
        a = fine_rows([(a_ref, FIRST), (a2_ref, SECOND)], t)
        b = deep_rows([(b_ref, FIRST), (b2_ref, SECOND)], t)
        left, right = one_side(odd_core, get_rows(near_ref, 0, PLANES, 3, t))
        smooth, detail = lift(left, a, right)
        for c in range(PAIRS):
            ya_ref[t, pl.ds(c, PLANES, stride=16), :] = smooth[c]
            ya_ref[t, pl.ds(8 + c, PLANES, stride=16), :] = detail[c]
        left, right = one_side(odd_core, low_halo(halo_ref, t))
        smooth, _ = lift(left, b, right)
        left, right = one_side(odd_core, get_rows(near_ref, 36, PAIRS, 3, t))
        to_right, to_left = coarse_terms(b)
        rows = smooth + plus(left, edge_right(to_left)) + plus(right, edge_left(to_right))
        for j, row in enumerate(rows):
            s_ref[t, pl.ds(8 * j, PAIRS), :] = row


def middle_kernel(near_ya_ref, s_ref, other_ref, far_ref, low_ref, ya_ref, yb_ref, xnear_ref, xother_ref, xfar_ref, xfar2_ref, halo_ref):
    odd_core = lax.axis_index("span") % 2 == 1
    odd_x = lax.axis_index("stream") % 2 == 1
    odd_pair = lax.axis_index("stream") // 2 % 2 == 1
    low_rows(other_ref, low_ref, halo_ref)
    for t in range(TILES):
        right, left = one_side(odd_core, get_rows(other_ref, 0, PLANES, 3, t))
        smooth, detail = lift(left, [None] * ROWS, right)
        for start, terms in ((0, smooth), (8, detail)):
            for c, term in enumerate(terms):
                rows = pl.ds(start + c, PLANES, stride=16)
                if term is not None:
                    ya_ref[t, rows, :] = near_ya_ref[t, rows, :] + term
                else:
                    ya_ref[t, rows, :] = near_ya_ref[t, rows, :]
        held = [s_ref[t, pl.ds(8 * j, PAIRS), :] for j in range(12)]
        right, left = one_side(odd_core, low_halo(halo_ref, t))
        terms, _ = lift(left, [None] * ROWS, right)
        smooth = plus(held[:6], terms)
        right, left = one_side(odd_core, get_rows(other_ref, 36, PAIRS, 3, t))
        one, two = get_rows(far_ref, 0, PAIRS, 2, t)
        zero = jnp.zeros_like(one)
        left = plus(plus(left, held[6:9]), choose(odd_core, [one, zero, two], [zero, zero, zero]))
        right = plus(plus(right, held[9:12]), choose(odd_core, [zero, zero, zero], [zero, one, zero]))
        smooth, detail = lift(left, smooth, right)
        for c, row in enumerate(interleaved(smooth, detail)):
            yb_ref[t, pl.ds(c, PAIRS, stride=8), :] = row
    for t in range(TILES):
        a = stream_planes(ya_ref, t)
        right, left = edge_right(a), edge_left(a)
        for ref, planes in ((xnear_ref, choose(odd_x, left, right)), (xother_ref, choose(odd_x, right, left))):
            put_rows(ref, 0, [half for plane in planes for half in (plane[0:6], plane[8:14])], t)
    for t in range(4):
        b = low_planes(yb_ref, t)
        smooth, _ = lift(None, b, None)
        to_right, to_left = coarse_terms(b)
        for half, planes in ((0, b), (4, smooth)):
            right, left = edge_right(planes), edge_left(planes)
            put_rows(xnear_ref, 36, [plane[0:6] for plane in choose(odd_x, left, right)], t + half)
            put_rows(xother_ref, 36, [plane[0:6] for plane in choose(odd_x, right, left)], t + half)
        far_right, far_left = edge_right(to_right), edge_left(to_left)
        far_right, far_left = [far_right[0], far_right[2]], [far_left[1], jnp.zeros_like(far_left[1])]
        for half in (0, 1):
            put_rows(xfar_ref, 0, [choose(odd_pair, far_left, far_right)[half][0:6]], t + 4 * half)
            put_rows(xfar2_ref, 0, [choose(odd_pair, far_right, far_left)[half][0:6]], t + 4 * half)


def stream_planes(ya_ref, t):
    return [ya_ref[t, pl.ds(16 * x, 16), :] for x in range(PLANES)]


def low_planes(yb_ref, t):
    return [yb_ref[t + 4 * odd, pl.ds(8 * k, 8), :] for k in range(PAIRS) for odd in (0, 1)]


def rows_of(x, y, t):
    return pl.ds((x * ROWS + y) * TILES + t, PAIRS, stride=2 * TILES)


def own_kernel(ya_ref, yb_ref, part_ref, s_ref):
    for t in range(TILES):
        for x, plane in enumerate(interleaved(*lift(None, stream_planes(ya_ref, t), None))):
            part_ref[rows_of(x, 0, t), :] = plane[0:6]
            part_ref[rows_of(x, 1, t), :] = plane[8:14]
    for t in range(4):
        b = low_planes(yb_ref, t)
        smooth, _ = lift(None, b, None)
        to_right, to_left = coarse_terms(b)
        for j, row in enumerate(smooth + edge_right(to_left) + edge_left(to_right)):
            s_ref[t, pl.ds(8 * j, 8), :] = row


def last_kernel(part_ref, s_ref, xnear_ref, xother_ref, xfar_ref, xfar2_ref, out_ref, c_ref, o_ref, sems):
    odd_x = lax.axis_index("stream") % 2 == 1
    odd_pair = lax.axis_index("stream") // 2 % 2 == 1

    def leave(ref, x):
        rows = pl.ds(x * ROWS * TILES, ROWS * TILES)
        copy = pltpu.make_async_copy(ref.at[rows], out_ref.at[rows], sems.at[x])
        copy.start()
        return copy

    apart = (3, 5, 7)
    copies = [leave(part_ref, x) for x in apart]
    for t in range(TILES):
        near, other = (get_rows(ref, 0, 6, 6, t) for ref in (xnear_ref, xother_ref))
        left, right = choose(odd_x, near, other), choose(odd_x, other, near)
        for y in (0, 1):
            terms = interleaved(*lift(left[y::2], [None] * PLANES, right[y::2]))
            for x, term in enumerate(terms):
                if x not in apart:
                    rows = rows_of(x, y, t)
                    o_ref[rows, :] = total(part_ref[rows, :], term)
    copies += [leave(o_ref, x) for x in range(1, PLANES, 2) if x not in apart]
    for t in range(4):
        near, other = (get_rows(ref, 36, 6, 3, t) + get_rows(ref, 36, 6, 3, t + 4) for ref in (xnear_ref, xother_ref))
        far, far2 = (get_rows(ref, 0, 6, 1, t) + get_rows(ref, 0, 6, 1, t + 4) for ref in (xfar_ref, xfar2_ref))
        left, right = choose(odd_x, near, other), choose(odd_x, other, near)
        far_left, far_right = choose(odd_pair, far, far2), choose(odd_pair, far2, far)
        held = [s_ref[t, pl.ds(8 * j, 6), :] for j in range(12)]
        terms, _ = lift(left[:3], [None] * PLANES, right[:3])
        smooth = plus(held[:6], terms)
        left = plus(plus(left[3:], held[6:9]), [far_left[0], None, far_left[1]])
        right = plus(plus(right[3:], held[9:12]), [None, far_right[0], None])
        for k, plane in enumerate(interleaved(*lift(left, smooth, right))):
            c_ref[pl.ds(8 * k, 6), cut(t)] = plane
    i, j = (lax.broadcasted_iota(jnp.int32, (LANES, 2 * LANES), axis) for axis in (0, 1))
    spread = jnp.where(j == 2 * i, 1.0, 0.0).astype(jnp.bfloat16)
    even = (lane((6, LANES)) & 1) == 0
    split = parts(c_ref[...])
    for t in range(0, TILES, 2):
        wide = sum(
            jnp.dot(p[:, t * 64:t * 64 + LANES], spread, preferred_element_type=jnp.float32) for p in split
        )
        for half in (0, 1):
            for k in range(PAIRS):
                rows = rows_of(2 * k, 0, t + half)
                coarse = wide[8 * k:8 * k + 6, half * LANES:(half + 1) * LANES]
                o_ref[rows, :] = jnp.where(even, coarse, o_ref[rows, :])
    copies += [leave(o_ref, x) for x in range(0, PLANES, 2)]
    for copy in copies:
        copy.wait()


VMEM = pl.BlockSpec(memory_space=pltpu.VMEM)
HBM = pl.BlockSpec(memory_space=pltpu.HBM)


def call(kernel, shapes, args, scratch=(), sems=0, out=VMEM, kind=jnp.float32, cost=None):
    return pl.pallas_call(
        kernel,
        out_shape=[jax.ShapeDtypeStruct(s, kind) for s in shapes],
        in_specs=[VMEM] * len(args),
        out_specs=[out] + [VMEM] * (len(shapes) - 1),
        scratch_shapes=[pltpu.VMEM(s, jnp.float32) for s in scratch] + [pltpu.SemaphoreType.DMA((sems,))] * (sems > 0),
        compiler_params=pltpu.CompilerParams(vmem_limit_bytes=16 << 20),
        cost_estimate=cost,
    )(*args)


def message(count):
    return (TILES * count, LANES)


def local(streams, spans, fields):
    shape = fields.shape

    def send(rows, target):
        pairs = [(s * spans + y, (lambda q: q[0] % streams * spans + q[1] % spans)(target(s, y))) for s in range(streams) for y in range(spans)]
        return lax.ppermute(rows, ("stream", "span"), pairs)

    cost = pl.CostEstimate(flops=10**9, bytes_accessed=10**6, transcendentals=0)
    fine, low = call(table_kernel, [(4 * LANES, 2 * LANES), (6 * LANES, 2 * LANES)], [], kind=jnp.bfloat16, cost=cost)
    block = (PLANES * ROWS * TILES, LANES)
    fields = fields.reshape(block)
    shapes = lambda ys: [(TILES, PLANES * len(ys), LANES), (TILES // 2, PLANES * len(ys), LANES)]
    a, b, behind, far = call(first_kernel, shapes(FIRST) + [message(Y_FAR)] * 2, [fields, fine, low])
    behind = send(behind, lambda s, y: (s, y ^ 1))
    far = send(far, lambda s, y: (s, y + (2 if y % 2 else -2)))
    a2, b2, near, other = call(
        second_kernel, shapes(SECOND) + [message(EDGE)] * 2, [fields, fine, low, a, b], cost=cost
    )
    other, near = call(fold_kernel, [message(EDGE)] * 2, [other, behind, near])
    near = send(near, lambda s, y: (s, y ^ 1))
    other = send(other, lambda s, y: (s, y + (1 if y % 2 else -1)))
    ya, smooth = call(
        near_kernel,
        [(TILES, PLANES * 16, LANES), (TILES, 96, LANES)],
        [a, b, a2, b2, near, low],
        [(4, 48, LANES)],
        cost=cost,
    )
    ya, yb, xnear, xother, xfar, xfar2 = call(
        middle_kernel,
        [(TILES, PLANES * 16, LANES), (TILES, PAIRS * 8, LANES), message(EDGE), message(EDGE), message(X_FAR), message(X_FAR)],
        [ya, smooth, other, far, low],
        [(4, 48, LANES)],
    )
    xnear = send(xnear, lambda s, y: (s ^ 1, y))
    xother = send(xother, lambda s, y: (s + (1 if s % 2 else -1), y))
    xfar = send(xfar, lambda s, y: (s + (-2 if s // 2 % 2 else 2), y))
    xfar2 = send(xfar2, lambda s, y: (s + (2 if s // 2 % 2 else -2), y))
    part, smooth = call(own_kernel, [block, (4, 96, LANES)], [ya, yb], cost=cost)
    (out,) = call(
        last_kernel,
        [block],
        [part, smooth, xnear, xother, xfar, xfar2],
        [(48, CELLS // 2), block],
        sems=PLANES,
        out=HBM,
    )
    return out.reshape(shape)


def solution(mesh):
    return jax.shard_map(
        functools.partial(local, mesh.shape["stream"], mesh.shape["span"]),
        mesh=mesh,
        in_specs=(P(None, "stream", "span", None),),
        out_specs=P(None, "stream", "span", None),
        check_vma=False,
    )
```
